128 devices in a mesh: blk: 8 (over x, z_lo), bcast: 16 (over z_hi, y, core).
Axes of the slice: x: 4, y: 4, z: 4 (z_hi: 2, z_lo: 2; z = z_hi * 2 + z_lo), core: 2. Of those that a mesh axis runs over, the one named last changes fastest.
Arguments:
- coupling: float32 [8192, 4096], P('blk', 'bcast'), may hold values from -6 to 6
- denominators: float32 [8192, 4096], P('blk', 'bcast'), may hold values from 1.5 to 6
- integrals: bfloat16 [4096, 4096], P('bcast', 'blk'), may hold values from -0.125 to 0.125
- tile_sizes: int32 [32], replicated, may hold values from 64 to 128, as said below
- screen_ov: int32 [64, 32], replicated, may hold values 0 or 1
- screen_vv: int32 [32, 32], replicated, may hold values 0 or 1
Outputs:
- amplitudes: float32 [8192, 4096], P('blk', 'bcast')
The draws below stay inside these ranges and needn't reach their ends.
Inputs may be any that keep to these rules, and one draw needn't show every extreme that they name: `tile_sizes`: each pair tile has between 64 and 128 live pairs; some tile has exactly 128 and some exactly 64.
All inputs are finite; a program needn't handle non-finite values.
Results may differ from the reference program's by a relative error of at most 0.0012.
Values may be sent and summed in bfloat16 or wider, within the bound.
A program may use at most 64 MiB of HBM per device.

```python
import math
import jax
import jax.numpy as jnp

TILE = 128
ROW_TILE = 128
ITERS = 3
Q = 32
QT = 4096
P_SIZE = 8192


def draw_tile_sizes(key, part):
    key = jax.random.fold_in(key, 5)
    first, second = jax.random.split(key)
    sizes = jax.random.randint(first, (Q,), TILE // 2, TILE + 1)
    order = jax.random.permutation(second, Q)
    sizes = jnp.where(order == 0, TILE, sizes)
    sizes = jnp.where(order == 1, TILE // 2, sizes)
    return sizes.astype(jnp.int32)


def touch_ends(array, key, least, high):
    longest = array.shape.index(max(array.shape))
    spots = []
    for shift in (0, 1):
        where = [jax.random.randint(jax.random.fold_in(key, axis), (), 0, length) for axis, length in enumerate(array.shape)]
        where[longest] = (where[longest] + shift) % array.shape[longest]
        spots.append(tuple(where))
    return array.at[spots[0]].set(least).at[spots[1]].set(high)


def levels(rng, extent, cuts, least, top_value):
    def one(dim, parts):
        heights = jax.random.uniform(jax.random.fold_in(jax.random.fold_in(rng, 6), dim), (parts,), jnp.float32, least / len(cuts), top_value / len(cuts))
        return jnp.repeat(jnp.exp(heights), extent[dim] // parts).reshape((-1,) + (1,) * (len(extent) - dim - 1))

    factor_of = one(*cuts[0])
    for cut in cuts[1:]:
        factor_of = factor_of * one(*cut)
    return factor_of


def centred(stream_key, shape, spread, most, cuts=(), held_as=jnp.bfloat16):
    result = spread * jax.random.normal(stream_key, shape, jnp.float32)
    if cuts:
        result = result * levels(stream_key, shape, cuts, -0.22, 0.18)
    return jnp.clip(result, -most, most).astype(held_as)


def setup_inputs(seed: int = 0) -> dict:
    streams_of = jax.random.split(jax.random.key(seed), 7)
    return {
        "coupling": centred(streams_of[0], (P_SIZE, QT), 1.0, 6.0, ((0, 8), (1, 16)), jnp.float32),
        "denominators": jnp.clip(jnp.exp(math.log(6.0) - 1.3862944 * jax.random.uniform(streams_of[1], (P_SIZE, QT), jnp.float32) ** levels(streams_of[1], (P_SIZE, QT), ((0, 8), (1, 16)), -0.2, 0.2)), 1.5, 6.0),
        "integrals": centred(streams_of[2], (QT, QT), (QT // 2) ** -0.5, 0.125, ((0, 16), (1, 8))),
        "tile_sizes": draw_tile_sizes(jax.random.fold_in(streams_of[6], 71), 0),
        "screen_ov": touch_ends((jax.random.randint(streams_of[4], (P_SIZE // ROW_TILE, Q), 0, 4) < 3).astype(jnp.int32), jax.random.fold_in(streams_of[4], 1), 0, 1),
        "screen_vv": touch_ends((jax.random.randint(streams_of[5], (Q, Q), 0, 4) < 3).astype(jnp.int32), jax.random.fold_in(streams_of[5], 1), 0, 1),
    }


def build_keep(tile_sizes, screen_ov):
    live = (jnp.arange(TILE)[None, :] < tile_sizes[:, None]).astype(jnp.float32)
    block = screen_ov.astype(jnp.float32)[:, None, :, None] * live[None, None, :, :]
    return jnp.broadcast_to(block, (P_SIZE // ROW_TILE, ROW_TILE, Q, TILE)).reshape(P_SIZE, QT)


def reference(coupling, denominators, integrals, tile_sizes, screen_ov, screen_vv):
    keep = build_keep(tile_sizes, screen_ov)
    screened = (integrals.reshape(Q, TILE, Q, TILE) * screen_vv.astype(jnp.bfloat16)[:, None, :, None]).reshape(QT, QT)
    amplitudes = coupling * keep / denominators
    for step in range(ITERS):
        rounded = amplitudes.astype(jnp.bfloat16)
        ladder = jnp.dot(rounded, screened.T, preferred_element_type=jnp.float32)
        amplitudes = (coupling + ladder) * keep / denominators
    return amplitudes
```

```python
import jax
import jax.numpy as jnp
from jax import lax
from jax.experimental import pallas as pl
from jax.experimental.pallas import tpu as pltpu
from jax.sharding import PartitionSpec as P

TILE = 128
ROW_TILE = 128
ITERS = 3
MESH = pl.DeviceIdType.MESH

ROWS = 1024
COLS = 256
CHUNK = 128
CHUNKS = ROWS // CHUNK
STEPS = ITERS * CHUNKS
HALF = CHUNK // 2
FINAL = 3
FORWARD = 5
RING = 4


def device(x, y, z, core):
    x, y, z, core = x % 4, y % 4, z % 4, core % 2
    return (x * 2 + z % 2, ((z // 2) * 4 + y) * 2 + core)


def kernel(
    sizes_ref,
    ov_ref,
    vv_ref,
    coupling_ref,
    den_ref,
    integrals_ref,
    out_ref,
    weight,
    amp,
    mine,
    table,
    sib_out,
    own,
    sib_in,
    z_out,
    z_in,
    up_send,
    down_send,
    up_recv,
    down_recv,
    fup_send,
    fdown_send,
    fup_recv,
    fdown_recv,
    sib_send,
    sib_recv,
    z_send,
    z_recv,
    t_send,
    t_recv,
):
    blk = lax.axis_index("blk")
    bcast = lax.axis_index("bcast")
    x, zl = blk // 2, blk % 2
    zh, y, core = bcast // 8, (bcast // 2) % 4, bcast % 2
    z = zh * 2 + zl
    up = device(x, y + 1, z, core)
    down = device(x, y + 3, z, core)
    sibling = device(x, y, z, core + 1)
    across = device(x, y, z + 2, core)
    inside = (x // 2) == zh

    barrier = pltpu.get_barrier_semaphore()

    def greet(dev):
        pl.semaphore_signal(barrier, inc=1, device_id=dev, device_id_type=MESH)

    for dev in (up, down, sibling, across):
        greet(dev)
    for i in range(2):
        for dz in range(4):
            for dc in range(2):
                source = device(2 * zh + (x % 2 + i) % 2, y, z + dz, core + dc)
                if i == 0 and dz == 0 and dc == 0:
                    pl.when(jnp.logical_not(inside))(lambda s=source: greet(s))
                else:
                    greet(source)

    for h in range(2):
        for j in range(2):
            for i in range(2):
                keep = vv_ref[bcast * 2 + i, blk * 4 + h * 2 + j].astype(jnp.float32)
                part = integrals_ref[
                    pl.ds(i * TILE, TILE), pl.ds((h * 2 + j) * TILE, TILE)
                ].astype(jnp.float32)
                mine[h, pl.ds(j * TILE, TILE), pl.ds(i * TILE, TILE)] = (
                    jnp.transpose(part * keep).astype(jnp.bfloat16)
                )

    size0 = sizes_ref[bcast * 2]
    size1 = sizes_ref[bcast * 2 + 1]

    def rows_of(k):
        return pl.ds(pl.multiple_of(k * CHUNK, CHUNK), CHUNK)

    def first_amplitudes(k):
        lane = lax.broadcasted_iota(jnp.int32, (CHUNK, COLS), 1)
        ov0 = ov_ref[blk * CHUNKS + k, bcast * 2]
        ov1 = ov_ref[blk * CHUNKS + k, bcast * 2 + 1]
        live0 = jnp.where(lane < size0, ov0, 0)
        live1 = jnp.where(lane - TILE < size1, ov1, 0)
        keep = jnp.where(lane < TILE, live0, live1).astype(jnp.float32)
        w = keep / den_ref[rows_of(k), :]
        weight[rows_of(k), :] = w
        amp[0, y, rows_of(k), :] = (coupling_ref[rows_of(k), :] * w).astype(jnp.bfloat16)

    def part_of(t, owner, k, offset, length):
        start = pl.multiple_of(k * CHUNK + offset, HALF)
        return amp.at[t, owner, pl.ds(start, length), :]

    def remote(ref, target, send, recv):
        return pltpu.make_async_remote_copy(
            src_ref=ref, dst_ref=ref, send_sem=send, recv_sem=recv,
            device_id=target, device_id_type=MESH,
        )

    def send_up(s):
        ref = part_of(s // CHUNKS, y, s % CHUNKS, 0, CHUNK)
        return remote(ref, up, up_send.at[s], up_recv.at[s])

    def send_down(s):
        ref = part_of(s // CHUNKS, y, s % CHUNKS, 0, CHUNK)
        return remote(ref, down, down_send.at[s], down_recv.at[s])

    below, above, far = (y + 3) % RING, (y + 1) % RING, (y + 2) % RING

    def from_below(s):
        ref = part_of(s // CHUNKS, below, s % CHUNKS, 0, CHUNK)
        return remote(ref, up, up_send.at[s], up_recv.at[s])

    def from_above(s):
        ref = part_of(s // CHUNKS, above, s % CHUNKS, 0, CHUNK)
        return remote(ref, down, down_send.at[s], down_recv.at[s])

    def pass_up(s):
        ref = part_of(s // CHUNKS, below, s % CHUNKS, 0, HALF)
        return remote(ref, up, fup_send.at[s], fup_recv.at[s])

    def pass_down(s):
        ref = part_of(s // CHUNKS, above, s % CHUNKS, HALF, HALF)
        return remote(ref, down, fdown_send.at[s], fdown_recv.at[s])

    def far_from_below(s):
        ref = part_of(s // CHUNKS, far, s % CHUNKS, 0, HALF)
        return remote(ref, up, fup_send.at[s], fup_recv.at[s])

    def far_from_above(s):
        ref = part_of(s // CHUNKS, far, s % CHUNKS, HALF, HALF)
        return remote(ref, down, fdown_send.at[s], fdown_recv.at[s])

    def to_sibling(s):
        return pltpu.make_async_remote_copy(
            src_ref=sib_out.at[s % CHUNKS], dst_ref=sib_in.at[s],
            send_sem=sib_send.at[s], recv_sem=sib_recv.at[s],
            device_id=sibling, device_id_type=MESH,
        )

    def to_across(s):
        return pltpu.make_async_remote_copy(
            src_ref=z_out.at[s % CHUNKS], dst_ref=z_in.at[s],
            send_sem=z_send.at[s], recv_sem=z_recv.at[s],
            device_id=across, device_id_type=MESH,
        )

    def start_ring(s):
        send_up(s).start()
        send_down(s).start()

    def forward(s):
        from_below(s).wait_recv()
        pass_up(s).start()
        from_above(s).wait_recv()
        pass_down(s).start()

    def product(s):
        far_from_below(s).wait_recv()
        far_from_above(s).wait_recv()
        t, k = s // CHUNKS, s % CHUNKS
        lhs = jnp.concatenate([amp[t, o, rows_of(k), :] for o in range(RING)], axis=1)
        for h in range(2):
            sib_out[k, h] = jnp.dot(
                lhs, table[h * 2 + (1 - core)], preferred_element_type=jnp.float32
            )
        to_sibling(s).start()
        for h in range(2):
            own[k, h] = jnp.dot(
                lhs, table[h * 2 + core], preferred_element_type=jnp.float32
            )

    def reduce_core(s):
        k = s % CHUNKS
        to_sibling(s).wait()
        z_out[k] = (own[k, 1 - zh] + sib_in[s, 1 - zh]).astype(jnp.bfloat16)
        to_across(s).start()

    def finish(s):
        t, k = s // CHUNKS, s % CHUNKS
        to_across(s).wait()
        ladder = own[k, zh] + sib_in[s, zh] + z_in[s].astype(jnp.float32)
        value = (coupling_ref[rows_of(k), :] + ladder) * weight[rows_of(k), :]

        @pl.when(t < ITERS - 1)
        def _():
            amp[t + 1, y, rows_of(k), :] = value.astype(jnp.bfloat16)
            start_ring(s + CHUNKS)

        @pl.when(t == ITERS - 1)
        def _():
            out_ref[rows_of(k), :] = value

        send_up(s).wait_send()
        send_down(s).wait_send()
        pass_up(s).wait_send()
        pass_down(s).wait_send()

    first_amplitudes(0)
    pl.semaphore_wait(barrier, 20 - inside.astype(jnp.int32))
    start_ring(0)

    block = zh * 2 + core
    place = (x % 2) * 2 + zl
    landing = pl.ds(pl.multiple_of(place * COLS, COLS), COLS)
    sends = []
    for dx in range(4):
        for dl in range(2):
            for dc in range(2):
                n = dx * 4 + dl * 2 + dc
                target = device(x + dx, y, 2 * (x // 2) + (zl + dl) % 2, core + dc)
                copy = pltpu.make_async_remote_copy(
                    src_ref=mine.at[(core + dc) % 2],
                    dst_ref=table.at[block, landing, :],
                    send_sem=t_send.at[n],
                    recv_sem=t_recv.at[block * 4 + place],
                    device_id=target,
                    device_id_type=MESH,
                )
                sends.append(copy)
    local = pltpu.make_async_copy(
        mine.at[core], table.at[block, landing, :], t_recv.at[block * 4 + place]
    )
    for n, copy in enumerate(sends):
        if n == 0:
            pl.when(inside)(local.start)
            pl.when(jnp.logical_not(inside))(copy.start)
        else:
            copy.start()

    @pl.loop(1, CHUNKS)
    def _(k):
        first_amplitudes(k)
        start_ring(k)

    @pl.loop(0, CHUNKS)
    def _(k):
        forward(k)

    @pl.loop(0, 16)
    def _(n):
        ref = table.at[n // 4, pl.ds(pl.multiple_of((n % 4) * COLS, COLS), COLS), :]
        pltpu.make_async_remote_copy(
            src_ref=ref, dst_ref=ref, send_sem=t_send.at[n], recv_sem=t_recv.at[n],
            device_id=sibling, device_id_type=MESH,
        ).wait_recv()

    @pl.loop(0, STEPS + FINAL)
    def _(tick):
        @pl.when(jnp.logical_and(tick >= FINAL, tick < STEPS + FINAL))
        def _():
            finish(tick - FINAL)

        @pl.when(jnp.logical_and(tick >= FORWARD, tick < STEPS - CHUNKS + FORWARD))
        def _():
            forward(tick - FORWARD + CHUNKS)

        @pl.when(jnp.logical_and(tick >= 1, tick < STEPS + 1))
        def _():
            reduce_core(tick - 1)

        @pl.when(tick < STEPS)
        def _():
            product(tick)

    pl.when(jnp.logical_not(inside))(sends[0].wait_send)
    for copy in sends[1:]:
        copy.wait_send()


def local(coupling, denominators, integrals, tile_sizes, screen_ov, screen_vv):
    dma = pltpu.SemaphoreType.DMA
    smem = pl.BlockSpec(memory_space=pltpu.SMEM)
    vmem = pl.BlockSpec(memory_space=pltpu.VMEM)
    return pl.pallas_call(
        kernel,
        out_shape=jax.ShapeDtypeStruct((ROWS, COLS), jnp.float32),
        in_specs=[smem] * 3 + [vmem] * 3,
        out_specs=vmem,
        scratch_shapes=[
            pltpu.VMEM((ROWS, COLS), jnp.float32),
            pltpu.VMEM((ITERS, RING, ROWS, COLS), jnp.bfloat16),
            pltpu.VMEM((2, COLS, COLS), jnp.bfloat16),
            pltpu.VMEM((4, RING * COLS, COLS), jnp.bfloat16),
            pltpu.VMEM((CHUNKS, 2, CHUNK, COLS), jnp.float32),
            pltpu.VMEM((CHUNKS, 2, CHUNK, COLS), jnp.float32),
            pltpu.VMEM((STEPS, 2, CHUNK, COLS), jnp.float32),
            pltpu.VMEM((CHUNKS, CHUNK, COLS), jnp.bfloat16),
            pltpu.VMEM((STEPS, CHUNK, COLS), jnp.bfloat16),
        ]
        + [dma((STEPS,))] * 12
        + [dma((16,))] * 2,
        compiler_params=pltpu.CompilerParams(
            collective_id=0, has_side_effects=True, vmem_limit_bytes=48 * 1024 * 1024
        ),
        cost_estimate=pl.CostEstimate(
            flops=3 * 2 * ROWS * 1024 * 1024,
            bytes_accessed=4 * 1024 * 1024,
            transcendentals=0,
        ),
    )(tile_sizes, screen_ov, screen_vv, coupling, denominators, integrals)


def solution(mesh):
    in_specs = (P("blk", "bcast"), P("blk", "bcast"), P("bcast", "blk"), P(), P(), P())
    out_specs = P("blk", "bcast")
    return jax.shard_map(local, mesh=mesh, in_specs=in_specs, out_specs=out_specs, check_vma=False)
```

```python
import jax
import jax.numpy as jnp
from jax import lax
from jax.experimental import pallas as pl
from jax.experimental.pallas import tpu as pltpu
from jax.sharding import PartitionSpec as P

TILE = 128
ROW_TILE = 128
ITERS = 3
MESH = pl.DeviceIdType.MESH

ROWS = 1024
COLS = 256
CHUNK = 128
CHUNKS = ROWS // CHUNK
STEPS = ITERS * CHUNKS
HALF = CHUNK // 2
FINAL = 3
FORWARD = 5
RING = 4


def device(x, y, z, core):
    x, y, z, core = x % 4, y % 4, z % 4, core % 2
    return (x * 2 + z % 2, ((z // 2) * 4 + y) * 2 + core)


def kernel(
    sizes_ref,
    ov_ref,
    vv_ref,
    coupling_ref,
    den_ref,
    integrals_ref,
    out_ref,
    weight,
    amp,
    swap,
    unit,
    ring,
    table,
    sib_out,
    own,
    sib_in,
    z_out,
    z_in,
    up_send,
    down_send,
    up_recv,
    down_recv,
    fup_send,
    fdown_send,
    fup_recv,
    fdown_recv,
    sib_send,
    sib_recv,
    z_send,
    z_recv,
    swap_send,
    swap_recv,
    ring_send,
    ring_recv,
    o_send,
    s_send,
    t_recv,
):
    blk = lax.axis_index("blk")
    bcast = lax.axis_index("bcast")
    x, zl = blk // 2, blk % 2
    zh, y, core = bcast // 8, (bcast // 2) % 4, bcast % 2
    z = zh * 2 + zl
    up = device(x, y + 1, z, core)
    down = device(x, y + 3, z, core)
    sibling = device(x, y, z, core + 1)
    across = device(x, y, z + 2, core)
    x_pair, x_out = x + 1 - 2 * (x % 2), x - 1 + 2 * (x % 2)
    z_mate, z_next = z + 1 - 2 * zl, z - 1 + 2 * zl
    pair_x = device(x_pair, y, z, core)
    out_x = device(x_out + 4, y, z, core)
    pair_z = device(x, y, z_mate, core)
    out_z = device(x, y, z_next + 4, core)
    right = device(x + 1, y, z, core)
    left = device(x + 3, y, z, core)
    inside = (x // 2) == zh
    outside = jnp.logical_not(inside)

    barrier = pltpu.get_barrier_semaphore()
    for dev in (up, down, sibling, across, pair_x, out_x, pair_z, out_z):
        pl.semaphore_signal(barrier, inc=1, device_id=dev, device_id_type=MESH)

    def screened(h, ref):
        for j in range(2):
            for i in range(2):
                keep = vv_ref[bcast * 2 + i, blk * 4 + h * 2 + j].astype(jnp.float32)
                at = pl.ds(pl.multiple_of((h * 2 + j) * TILE, TILE), TILE)
                part = integrals_ref[pl.ds(i * TILE, TILE), at].astype(jnp.float32)
                ref[pl.ds(j * TILE, TILE), pl.ds(i * TILE, TILE)] = jnp.transpose(
                    part * keep
                ).astype(jnp.bfloat16)

    screened(1 - core, swap)
    screened(core, ring.at[x])

    size0 = sizes_ref[bcast * 2]
    size1 = sizes_ref[bcast * 2 + 1]

    def rows_of(k):
        return pl.ds(pl.multiple_of(k * CHUNK, CHUNK), CHUNK)

    def first_amplitudes(k):
        lane = lax.broadcasted_iota(jnp.int32, (CHUNK, COLS), 1)
        ov0 = ov_ref[blk * CHUNKS + k, bcast * 2]
        ov1 = ov_ref[blk * CHUNKS + k, bcast * 2 + 1]
        live0 = jnp.where(lane < size0, ov0, 0)
        live1 = jnp.where(lane - TILE < size1, ov1, 0)
        keep = jnp.where(lane < TILE, live0, live1).astype(jnp.float32)
        w = keep / den_ref[rows_of(k), :]
        weight[rows_of(k), :] = w
        amp[0, y, rows_of(k), :] = (coupling_ref[rows_of(k), :] * w).astype(jnp.bfloat16)

    def part_of(t, owner, k, offset, length):
        start = pl.multiple_of(k * CHUNK + offset, HALF)
        return amp.at[t, owner, pl.ds(start, length), :]

    def remote(ref, target, send, recv):
        return pltpu.make_async_remote_copy(
            src_ref=ref, dst_ref=ref, send_sem=send, recv_sem=recv,
            device_id=target, device_id_type=MESH,
        )

    def send_up(s):
        ref = part_of(s // CHUNKS, y, s % CHUNKS, 0, CHUNK)
        return remote(ref, up, up_send.at[s], up_recv.at[s])

    def send_down(s):
        ref = part_of(s // CHUNKS, y, s % CHUNKS, 0, CHUNK)
        return remote(ref, down, down_send.at[s], down_recv.at[s])

    below, above, far = (y + 3) % RING, (y + 1) % RING, (y + 2) % RING

    def from_below(s):
        ref = part_of(s // CHUNKS, below, s % CHUNKS, 0, CHUNK)
        return remote(ref, up, up_send.at[s], up_recv.at[s])

    def from_above(s):
        ref = part_of(s // CHUNKS, above, s % CHUNKS, 0, CHUNK)
        return remote(ref, down, down_send.at[s], down_recv.at[s])

    def pass_up(s):
        ref = part_of(s // CHUNKS, below, s % CHUNKS, 0, HALF)
        return remote(ref, up, fup_send.at[s], fup_recv.at[s])

    def pass_down(s):
        ref = part_of(s // CHUNKS, above, s % CHUNKS, HALF, HALF)
        return remote(ref, down, fdown_send.at[s], fdown_recv.at[s])

    def far_from_below(s):
        ref = part_of(s // CHUNKS, far, s % CHUNKS, 0, HALF)
        return remote(ref, up, fup_send.at[s], fup_recv.at[s])

    def far_from_above(s):
        ref = part_of(s // CHUNKS, far, s % CHUNKS, HALF, HALF)
        return remote(ref, down, fdown_send.at[s], fdown_recv.at[s])

    def to_sibling(s):
        return pltpu.make_async_remote_copy(
            src_ref=sib_out.at[s % CHUNKS], dst_ref=sib_in.at[s],
            send_sem=sib_send.at[s], recv_sem=sib_recv.at[s],
            device_id=sibling, device_id_type=MESH,
        )

    def to_across(s):
        return pltpu.make_async_remote_copy(
            src_ref=z_out.at[s % CHUNKS], dst_ref=z_in.at[s],
            send_sem=z_send.at[s], recv_sem=z_recv.at[s],
            device_id=across, device_id_type=MESH,
        )

    def start_ring(s):
        send_up(s).start()
        send_down(s).start()

    def forward(s):
        from_below(s).wait_recv()
        pass_up(s).start()
        from_above(s).wait_recv()
        pass_down(s).start()

    def product(s):
        far_from_below(s).wait_recv()
        far_from_above(s).wait_recv()
        t, k = s // CHUNKS, s % CHUNKS
        lhs = jnp.concatenate([amp[t, o, rows_of(k), :] for o in range(RING)], axis=1)
        for h in range(2):
            sib_out[k, h] = jnp.dot(
                lhs, table[h * 2 + (1 - core)], preferred_element_type=jnp.float32
            )
        to_sibling(s).start()
        for h in range(2):
            own[k, h] = jnp.dot(
                lhs, table[h * 2 + core], preferred_element_type=jnp.float32
            )

    def reduce_core(s):
        k = s % CHUNKS
        to_sibling(s).wait()
        z_out[k] = (own[k, 1 - zh] + sib_in[s, 1 - zh]).astype(jnp.bfloat16)
        to_across(s).start()

    def finish(s):
        t, k = s // CHUNKS, s % CHUNKS
        to_across(s).wait()
        ladder = own[k, zh] + sib_in[s, zh] + z_in[s].astype(jnp.float32)
        value = (coupling_ref[rows_of(k), :] + ladder) * weight[rows_of(k), :]

        @pl.when(t < ITERS - 1)
        def _():
            amp[t + 1, y, rows_of(k), :] = value.astype(jnp.bfloat16)
            start_ring(s + CHUNKS)

        @pl.when(t == ITERS - 1)
        def _():
            out_ref[rows_of(k), :] = value

        send_up(s).wait_send()
        send_down(s).wait_send()
        pass_up(s).wait_send()
        pass_down(s).wait_send()

    def slot_of(first_core, zh_of, parity, zl_of):
        return (zh_of * 2 + first_core) * 4 + parity * 2 + zl_of

    def at_slot(slot):
        start = pl.multiple_of((slot % 4) * COLS, COLS)
        return table.at[slot // 4, pl.ds(start, COLS), :]

    def unit_copy(src, slot, send, target):
        return pltpu.make_async_remote_copy(
            src_ref=src, dst_ref=at_slot(slot), send_sem=send, recv_sem=t_recv.at[slot],
            device_id=target, device_id_type=MESH,
        )

    def arrived(slot):
        unit_copy(at_slot(slot), slot, swap_send, sibling).wait_recv()

    to_swap = pltpu.make_async_remote_copy(
        src_ref=swap, dst_ref=unit, send_sem=swap_send, recv_sem=swap_recv,
        device_id=sibling, device_id_type=MESH,
    )
    parity = x % 2

    def ring_part(owner, half):
        owner = (owner + 4) % 4
        if half is None:
            return ring.at[owner]
        return ring.at[owner, pl.ds(half * TILE, TILE), :]

    def ring_copy(owner, half, n, target):
        ref = ring_part(owner, half)
        return remote(ref, target, ring_send.at[n], ring_recv.at[n])

    def o_slot(owner):
        return slot_of(core, zh, owner % 2, zl)

    def over_z(n):
        owner = (x + (0, 3, 1, 2)[n]) % 4
        target = tuple(
            jnp.where(owner // 2 == zh, a, b) for a, b in zip(pair_z, out_z)
        )
        return unit_copy(ring.at[owner], o_slot(owner), o_send.at[n], target)

    def o_pass(n):
        slot = slot_of(core, 1 - zh, n, 1 - zl)
        return unit_copy(at_slot(slot), slot, o_send.at[4 + n], pair_z)

    s_slots = [
        lambda par, a=a, b=b: slot_of(1 - core, a, par, b)
        for a, b in ((zh, zl), (zh, 1 - zl), (1 - zh, 1 - zl), (1 - zh, zl))
    ]
    first_target = tuple(jnp.where(inside, a, b) for a, b in zip(pair_z, out_z))
    s_first = unit_copy(unit, s_slots[0](parity), s_send.at[0], first_target)
    s_pass = unit_copy(
        at_slot(s_slots[2](parity)), s_slots[2](parity), s_send.at[1], pair_z
    )

    def s_inside(n, k):
        slot = s_slots[n](parity)
        src = unit if n == 0 else at_slot(slot)
        return unit_copy(src, slot, s_send.at[2 + 2 * n + k], (pair_x, out_x)[k])

    def s_outside(n):
        slot = s_slots[n](1 - parity)
        return unit_copy(at_slot(slot), slot, s_send.at[2 + 2 * n], pair_x)

    def s_start(n):
        s_inside(n, 1).start()
        s_inside(n, 0).start()

    def s_relay(n):
        arrived(s_slots[n](1 - parity))
        s_outside(n).start()

    def new_chunk(k):
        first_amplitudes(k)
        start_ring(k)

    first_amplitudes(0)
    pl.semaphore_wait(barrier, 8)
    to_swap.start()
    ring_copy(x, None, 0, right).start()
    ring_copy(x, None, 1, left).start()
    start_ring(0)
    over_z(0).start()
    new_chunk(1)

    to_swap.wait_recv()
    s_first.start()

    @pl.when(inside)
    def _():
        s_start(0)
        table[(zh * 2 + 1 - core), pl.ds(pl.multiple_of((parity * 2 + zl) * COLS, COLS), COLS), :] = unit[...]

    @pl.loop(2, 5)
    def _(k):
        new_chunk(k)

    ring_copy(x + 3, None, 0, right).wait_recv()
    ring_copy(x + 3, 0, 2, right).start()
    over_z(1).start()
    ring_copy(x + 1, None, 1, left).wait_recv()
    ring_copy(x + 1, 1, 3, left).start()
    over_z(2).start()

    @pl.loop(5, CHUNKS)
    def _(k):
        new_chunk(k)

    forward(0)

    @pl.when(inside)
    def _():
        arrived(s_slots[1](parity))
        s_start(1)
        arrived(s_slots[2](parity))
        s_pass.start()
        s_start(2)

    @pl.when(outside)
    def _():
        s_relay(0)

    ring_copy(x + 2, 0, 2, right).wait_recv()
    ring_copy(x + 2, 1, 3, left).wait_recv()
    over_z(3).start()
    for p in range(2):
        owner = 2 * zh + p
        table[zh * 2 + core, pl.ds(pl.multiple_of((p * 2 + zl) * COLS, COLS), COLS), :] = ring[owner]
    forward(1)
    forward(2)
    pl.when(outside)(lambda: s_relay(1))
    forward(3)

    @pl.when(inside)
    def _():
        arrived(s_slots[3](parity))
        s_start(3)

    pl.when(outside)(lambda: s_relay(2))
    for n in range(2):
        arrived(slot_of(core, 1 - zh, n, 1 - zl))
        o_pass(n).start()
        forward(4 + n)
    pl.when(outside)(lambda: s_relay(3))
    forward(6)
    forward(7)
    for n in range(2):
        arrived(slot_of(core, zh, n, 1 - zl))
        arrived(slot_of(core, 1 - zh, n, zl))
    for n in range(4):
        arrived(s_slots[n](jnp.where(inside, 1 - parity, parity)))

    @pl.loop(0, STEPS + FINAL)
    def _(tick):
        @pl.when(jnp.logical_and(tick >= FINAL, tick < STEPS + FINAL))
        def _():
            finish(tick - FINAL)

        @pl.when(jnp.logical_and(tick >= FORWARD, tick < STEPS - CHUNKS + FORWARD))
        def _():
            forward(tick - FORWARD + CHUNKS)

        @pl.when(jnp.logical_and(tick >= 1, tick < STEPS + 1))
        def _():
            reduce_core(tick - 1)

        @pl.when(tick < STEPS)
        def _():
            product(tick)

    to_swap.wait_send()
    for n, (owner, half) in enumerate(((x, None), (x, None), (x + 3, 0), (x + 1, 1))):
        ring_copy(owner, half, n, right).wait_send()
    for n in range(4):
        over_z(n).wait_send()
    o_pass(0).wait_send()
    o_pass(1).wait_send()
    s_first.wait_send()

    @pl.when(inside)
    def _():
        s_pass.wait_send()
        for n in range(4):
            for k in range(2):
                s_inside(n, k).wait_send()

    @pl.when(outside)
    def _():
        for n in range(4):
            s_outside(n).wait_send()


def local(coupling, denominators, integrals, tile_sizes, screen_ov, screen_vv):
    dma = pltpu.SemaphoreType.DMA
    smem = pl.BlockSpec(memory_space=pltpu.SMEM)
    vmem = pl.BlockSpec(memory_space=pltpu.VMEM)
    return pl.pallas_call(
        kernel,
        out_shape=jax.ShapeDtypeStruct((ROWS, COLS), jnp.float32),
        in_specs=[smem] * 3 + [vmem] * 3,
        out_specs=vmem,
        scratch_shapes=[
            pltpu.VMEM((ROWS, COLS), jnp.float32),
            pltpu.VMEM((ITERS, RING, ROWS, COLS), jnp.bfloat16),
            pltpu.VMEM((COLS, COLS), jnp.bfloat16),
            pltpu.VMEM((COLS, COLS), jnp.bfloat16),
            pltpu.VMEM((4, COLS, COLS), jnp.bfloat16),
            pltpu.VMEM((4, RING * COLS, COLS), jnp.bfloat16),
            pltpu.VMEM((CHUNKS, 2, CHUNK, COLS), jnp.float32),
            pltpu.VMEM((CHUNKS, 2, CHUNK, COLS), jnp.float32),
            pltpu.VMEM((STEPS, 2, CHUNK, COLS), jnp.float32),
            pltpu.VMEM((CHUNKS, CHUNK, COLS), jnp.bfloat16),
            pltpu.VMEM((STEPS, CHUNK, COLS), jnp.bfloat16),
        ]
        + [dma((STEPS,))] * 12
        + [dma, dma, dma((4,)), dma((4,)), dma((6,)), dma((10,)), dma((16,))],
        compiler_params=pltpu.CompilerParams(
            collective_id=0, has_side_effects=True, vmem_limit_bytes=48 * 1024 * 1024
        ),
        cost_estimate=pl.CostEstimate(
            flops=3 * 2 * ROWS * 1024 * 1024,
            bytes_accessed=4 * 1024 * 1024,
            transcendentals=0,
        ),
    )(tile_sizes, screen_ov, screen_vv, coupling, denominators, integrals)


def solution(mesh):
    in_specs = (P("blk", "bcast"), P("blk", "bcast"), P("bcast", "blk"), P(), P(), P())
    out_specs = P("blk", "bcast")
    return jax.shard_map(local, mesh=mesh, in_specs=in_specs, out_specs=out_specs, check_vma=False)
```

```python
import jax
import jax.numpy as jnp
from jax import lax
from jax.experimental import pallas as pl
from jax.experimental.pallas import tpu as pltpu
from jax.sharding import PartitionSpec as P

TILE = 128
ROW_TILE = 128
ITERS = 3
MESH = pl.DeviceIdType.MESH

ROWS = 1024
COLS = 256
CHUNK = 128
CHUNKS = ROWS // CHUNK
SPLIT = ROW_TILE // CHUNK
STEPS = ITERS * CHUNKS
HALF = CHUNK // 2
FINAL = 4
FORWARD = 6
RING = 4


def device(x, y, z, core):
    x, y, z, core = x % 4, y % 4, z % 4, core % 2
    return (x * 2 + z % 2, ((z // 2) * 4 + y) * 2 + core)


def kernel(
    sizes_hbm,
    ov_hbm,
    vv_hbm,
    coupling_hbm,
    den_hbm,
    integrals_hbm,
    out_ref,
    sizes_ref,
    ov_ref,
    vv_ref,
    coupling_ref,
    den_ref,
    integrals_ref,
    loaded,
    weight,
    amp,
    swap,
    unit,
    ring,
    table,
    sib_out,
    own,
    sib_in,
    z_out,
    z_in,
    up_send,
    down_send,
    up_recv,
    down_recv,
    fup_send,
    fdown_send,
    fup_recv,
    fdown_recv,
    sib_send,
    sib_recv,
    z_send,
    z_recv,
    swap_send,
    swap_recv,
    ring_send,
    ring_recv,
    o_send,
    s_send,
    t_recv,
):
    blk = lax.axis_index("blk")
    bcast = lax.axis_index("bcast")
    x, zl = blk // 2, blk % 2
    zh, y, core = bcast // 8, (bcast // 2) % 4, bcast % 2
    z = zh * 2 + zl
    up = device(x, y + 1, z, core)
    down = device(x, y + 3, z, core)
    sibling = device(x, y, z, core + 1)
    across = device(x, y, z + 2, core)
    x_pair, x_out = x + 1 - 2 * (x % 2), x - 1 + 2 * (x % 2)
    z_mate, z_next = z + 1 - 2 * zl, z - 1 + 2 * zl
    pair_x = device(x_pair, y, z, core)
    out_x = device(x_out + 4, y, z, core)
    pair_z = device(x, y, z_mate, core)
    out_z = device(x, y, z_next + 4, core)
    right = device(x + 1, y, z, core)
    left = device(x + 3, y, z, core)
    inside = (x // 2) == zh
    outside = jnp.logical_not(inside)

    loads = [
        pltpu.make_async_copy(src, dst, loaded.at[n])
        for n, (src, dst) in enumerate(
            (
                (vv_hbm, vv_ref),
                (integrals_hbm, integrals_ref),
                (sizes_hbm, sizes_ref),
                (ov_hbm, ov_ref),
                (coupling_hbm, coupling_ref),
                (den_hbm, den_ref),
            )
        )
    ]
    for load in loads:
        load.start()

    barrier = pltpu.get_barrier_semaphore()
    for dev in (up, down, sibling, across, pair_x, out_x, pair_z, out_z):
        pl.semaphore_signal(barrier, inc=1, device_id=dev, device_id_type=MESH)

    def screened(h, ref):
        for j in range(2):
            for i in range(2):
                keep = vv_ref[bcast * 2 + i, blk * 4 + h * 2 + j].astype(jnp.float32)
                at = pl.ds(pl.multiple_of((h * 2 + j) * TILE, TILE), TILE)
                part = integrals_ref[pl.ds(i * TILE, TILE), at].astype(jnp.float32)
                ref[pl.ds(j * TILE, TILE), pl.ds(i * TILE, TILE)] = jnp.transpose(
                    part * keep
                ).astype(jnp.bfloat16)

    loads[0].wait()
    loads[1].wait()
    screened(1 - core, swap)
    screened(core, ring.at[x])

    def rows_of(k):
        return pl.ds(pl.multiple_of(k * CHUNK, CHUNK), CHUNK)

    def first_amplitudes(k):
        lane = lax.broadcasted_iota(jnp.int32, (CHUNK, COLS), 1)
        size0, size1 = sizes_ref[bcast * 2], sizes_ref[bcast * 2 + 1]
        ov0 = ov_ref[bcast * 2, blk * 8 + k // SPLIT]
        ov1 = ov_ref[bcast * 2 + 1, blk * 8 + k // SPLIT]
        live0 = jnp.where(lane < size0, ov0, 0)
        live1 = jnp.where(lane - TILE < size1, ov1, 0)
        keep = jnp.where(lane < TILE, live0, live1).astype(jnp.float32)
        w = keep / den_ref[rows_of(k), :]
        weight[rows_of(k), :] = w
        amp[0, y, rows_of(k), :] = (coupling_ref[rows_of(k), :] * w).astype(jnp.bfloat16)

    def part_of(t, owner, k, offset, length):
        start = pl.multiple_of(k * CHUNK + offset, HALF)
        return amp.at[t, owner, pl.ds(start, length), :]

    def remote(ref, target, send, recv):
        return pltpu.make_async_remote_copy(
            src_ref=ref, dst_ref=ref, send_sem=send, recv_sem=recv,
            device_id=target, device_id_type=MESH,
        )

    def send_up(s):
        ref = part_of(s // CHUNKS, y, s % CHUNKS, 0, CHUNK)
        return remote(ref, up, up_send.at[s], up_recv.at[s])

    def send_down(s):
        ref = part_of(s // CHUNKS, y, s % CHUNKS, 0, CHUNK)
        return remote(ref, down, down_send.at[s], down_recv.at[s])

    below, above, far = (y + 3) % RING, (y + 1) % RING, (y + 2) % RING

    def from_below(s):
        ref = part_of(s // CHUNKS, below, s % CHUNKS, 0, CHUNK)
        return remote(ref, up, up_send.at[s], up_recv.at[s])

    def from_above(s):
        ref = part_of(s // CHUNKS, above, s % CHUNKS, 0, CHUNK)
        return remote(ref, down, down_send.at[s], down_recv.at[s])

    def pass_up(s):
        ref = part_of(s // CHUNKS, below, s % CHUNKS, 0, HALF)
        return remote(ref, up, fup_send.at[s], fup_recv.at[s])

    def pass_down(s):
        ref = part_of(s // CHUNKS, above, s % CHUNKS, HALF, HALF)
        return remote(ref, down, fdown_send.at[s], fdown_recv.at[s])

    def far_from_below(s):
        ref = part_of(s // CHUNKS, far, s % CHUNKS, 0, HALF)
        return remote(ref, up, fup_send.at[s], fup_recv.at[s])

    def far_from_above(s):
        ref = part_of(s // CHUNKS, far, s % CHUNKS, HALF, HALF)
        return remote(ref, down, fdown_send.at[s], fdown_recv.at[s])

    def to_sibling(s):
        return pltpu.make_async_remote_copy(
            src_ref=sib_out.at[s % CHUNKS], dst_ref=sib_in.at[s],
            send_sem=sib_send.at[s], recv_sem=sib_recv.at[s],
            device_id=sibling, device_id_type=MESH,
        )

    def to_across(s):
        return pltpu.make_async_remote_copy(
            src_ref=z_out.at[s % CHUNKS], dst_ref=z_in.at[s],
            send_sem=z_send.at[s], recv_sem=z_recv.at[s],
            device_id=across, device_id_type=MESH,
        )

    def start_ring(s):
        send_up(s).start()
        send_down(s).start()

    def forward(s):
        from_below(s).wait_recv()
        pass_up(s).start()
        from_above(s).wait_recv()
        pass_down(s).start()

    def product(s):
        far_from_below(s).wait_recv()
        far_from_above(s).wait_recv()
        t, k = s // CHUNKS, s % CHUNKS
        lhs = jnp.concatenate([amp[t, o, rows_of(k), :] for o in range(RING)], axis=1)
        for h in range(2):
            sib_out[k, h] = jnp.dot(
                lhs, table[h * 2 + (1 - core)], preferred_element_type=jnp.float32
            )
        to_sibling(s).start()
        for h in range(2):
            own[k, h] = jnp.dot(
                lhs, table[h * 2 + core], preferred_element_type=jnp.float32
            )

    def reduce_core(s):
        k = s % CHUNKS
        to_sibling(s).wait()
        z_out[k] = (own[k, 1 - zh] + sib_in[s, 1 - zh]).astype(jnp.bfloat16)
        to_across(s).start()

    def finish(s):
        t, k = s // CHUNKS, s % CHUNKS
        to_across(s).wait()
        ladder = own[k, zh] + sib_in[s, zh] + z_in[s].astype(jnp.float32)
        value = (coupling_ref[rows_of(k), :] + ladder) * weight[rows_of(k), :]

        @pl.when(t < ITERS - 1)
        def _():
            amp[t + 1, y, rows_of(k), :] = value.astype(jnp.bfloat16)
            start_ring(s + CHUNKS)

        @pl.when(t == ITERS - 1)
        def _():
            out_ref[rows_of(k), :] = value

        send_up(s).wait_send()
        send_down(s).wait_send()
        pass_up(s).wait_send()
        pass_down(s).wait_send()

    def slot_of(first_core, zh_of, parity, zl_of):
        return (zh_of * 2 + first_core) * 4 + parity * 2 + zl_of

    def at_slot(slot):
        start = pl.multiple_of((slot % 4) * COLS, COLS)
        return table.at[slot // 4, pl.ds(start, COLS), :]

    def unit_copy(src, slot, send, target):
        return pltpu.make_async_remote_copy(
            src_ref=src, dst_ref=at_slot(slot), send_sem=send, recv_sem=t_recv.at[slot],
            device_id=target, device_id_type=MESH,
        )

    def arrived(slot):
        unit_copy(at_slot(slot), slot, swap_send, sibling).wait_recv()

    to_swap = pltpu.make_async_remote_copy(
        src_ref=swap, dst_ref=unit, send_sem=swap_send, recv_sem=swap_recv,
        device_id=sibling, device_id_type=MESH,
    )
    parity = x % 2

    def ring_part(owner, half):
        owner = (owner + 4) % 4
        if half is None:
            return ring.at[owner]
        return ring.at[owner, pl.ds(half * TILE, TILE), :]

    def ring_copy(owner, half, n, target):
        ref = ring_part(owner, half)
        return remote(ref, target, ring_send.at[n], ring_recv.at[n])

    def o_slot(owner):
        return slot_of(core, zh, owner % 2, zl)

    def over_z(n):
        owner = (x + (0, 3, 1, 2)[n]) % 4
        target = tuple(
            jnp.where(owner // 2 == zh, a, b) for a, b in zip(pair_z, out_z)
        )
        return unit_copy(ring.at[owner], o_slot(owner), o_send.at[n], target)

    def o_pass(n):
        slot = slot_of(core, 1 - zh, n, 1 - zl)
        return unit_copy(at_slot(slot), slot, o_send.at[4 + n], pair_z)

    s_slots = [
        lambda par, a=a, b=b: slot_of(1 - core, a, par, b)
        for a, b in ((zh, zl), (zh, 1 - zl), (1 - zh, 1 - zl), (1 - zh, zl))
    ]
    first_target = tuple(jnp.where(inside, a, b) for a, b in zip(pair_z, out_z))
    s_first = unit_copy(unit, s_slots[0](parity), s_send.at[0], first_target)
    s_pass = unit_copy(
        at_slot(s_slots[2](parity)), s_slots[2](parity), s_send.at[1], pair_z
    )

    def s_inside(n, k):
        slot = s_slots[n](parity)
        src = unit if n == 0 else at_slot(slot)
        return unit_copy(src, slot, s_send.at[2 + 2 * n + k], (pair_x, out_x)[k])

    def s_outside(n):
        slot = s_slots[n](1 - parity)
        return unit_copy(at_slot(slot), slot, s_send.at[2 + 2 * n], pair_x)

    def s_start(n):
        s_inside(n, 1).start()
        s_inside(n, 0).start()

    def s_relay(n):
        arrived(s_slots[n](1 - parity))
        s_outside(n).start()

    def forwards(eighth):
        @pl.loop(eighth * (CHUNKS // 8), (eighth + 1) * (CHUNKS // 8))
        def _(k):
            forward(k)

    def new_chunk(k):
        first_amplitudes(k)
        start_ring(k)

    pl.semaphore_wait(barrier, 8)
    to_swap.start()
    ring_copy(x, None, 0, right).start()
    ring_copy(x, None, 1, left).start()
    over_z(0).start()
    for load in loads[2:]:
        load.wait()
    new_chunk(0)

    to_swap.wait_recv()
    s_first.start()

    @pl.when(inside)
    def _():
        s_start(0)
        table[(zh * 2 + 1 - core), pl.ds(pl.multiple_of((parity * 2 + zl) * COLS, COLS), COLS), :] = unit[...]

    @pl.loop(1, CHUNKS // 2)
    def _(k):
        new_chunk(k)

    ring_copy(x + 3, None, 0, right).wait_recv()
    ring_copy(x + 3, 0, 2, right).start()
    over_z(1).start()
    ring_copy(x + 1, None, 1, left).wait_recv()
    ring_copy(x + 1, 1, 3, left).start()
    over_z(2).start()

    @pl.loop(CHUNKS // 2, CHUNKS)
    def _(k):
        new_chunk(k)

    forwards(0)

    @pl.when(inside)
    def _():
        arrived(s_slots[1](parity))
        s_start(1)
        arrived(s_slots[2](parity))
        s_pass.start()
        s_start(2)

    @pl.when(outside)
    def _():
        s_relay(0)

    ring_copy(x + 2, 0, 2, right).wait_recv()
    ring_copy(x + 2, 1, 3, left).wait_recv()
    over_z(3).start()
    for p in range(2):
        owner = 2 * zh + p
        table[zh * 2 + core, pl.ds(pl.multiple_of((p * 2 + zl) * COLS, COLS), COLS), :] = ring[owner]
    forwards(1)
    forwards(2)
    pl.when(outside)(lambda: s_relay(1))
    forwards(3)

    @pl.when(inside)
    def _():
        arrived(s_slots[3](parity))
        s_start(3)

    pl.when(outside)(lambda: s_relay(2))
    for n in range(2):
        arrived(slot_of(core, 1 - zh, n, 1 - zl))
        o_pass(n).start()
        forwards(4 + n)
    pl.when(outside)(lambda: s_relay(3))
    forwards(6)
    forwards(7)
    for n in range(2):
        arrived(slot_of(core, zh, n, 1 - zl))
        arrived(slot_of(core, 1 - zh, n, zl))
    for n in range(4):
        arrived(s_slots[n](jnp.where(inside, 1 - parity, parity)))

    @pl.loop(0, STEPS + FINAL)
    def _(tick):
        @pl.when(jnp.logical_and(tick >= FINAL, tick < STEPS + FINAL))
        def _():
            finish(tick - FINAL)

        @pl.when(jnp.logical_and(tick >= FORWARD, tick < STEPS - CHUNKS + FORWARD))
        def _():
            forward(tick - FORWARD + CHUNKS)

        @pl.when(jnp.logical_and(tick >= 1, tick < STEPS + 1))
        def _():
            reduce_core(tick - 1)

        @pl.when(tick < STEPS)
        def _():
            product(tick)

    to_swap.wait_send()
    for n, (owner, half) in enumerate(((x, None), (x, None), (x + 3, 0), (x + 1, 1))):
        ring_copy(owner, half, n, right).wait_send()
    for n in range(4):
        over_z(n).wait_send()
    o_pass(0).wait_send()
    o_pass(1).wait_send()
    s_first.wait_send()

    @pl.when(inside)
    def _():
        s_pass.wait_send()
        for n in range(4):
            for k in range(2):
                s_inside(n, k).wait_send()

    @pl.when(outside)
    def _():
        for n in range(4):
            s_outside(n).wait_send()


def local(coupling, denominators, integrals, tile_sizes, screen_ov, screen_vv):
    dma = pltpu.SemaphoreType.DMA
    anywhere = pl.BlockSpec(memory_space=pl.ANY)
    vmem = pl.BlockSpec(memory_space=pltpu.VMEM)
    return pl.pallas_call(
        kernel,
        out_shape=jax.ShapeDtypeStruct((ROWS, COLS), jnp.float32),
        in_specs=[anywhere] * 6,
        out_specs=vmem,
        scratch_shapes=[
            pltpu.SMEM((32,), jnp.int32),
            pltpu.SMEM((32, 64), jnp.int32),
            pltpu.SMEM((32, 32), jnp.int32),
            pltpu.VMEM((ROWS, COLS), jnp.float32),
            pltpu.VMEM((ROWS, COLS), jnp.float32),
            pltpu.VMEM((COLS, 2 * COLS), jnp.bfloat16),
            dma((6,)),
            pltpu.VMEM((ROWS, COLS), jnp.float32),
            pltpu.VMEM((ITERS, RING, ROWS, COLS), jnp.bfloat16),
            pltpu.VMEM((COLS, COLS), jnp.bfloat16),
            pltpu.VMEM((COLS, COLS), jnp.bfloat16),
            pltpu.VMEM((4, COLS, COLS), jnp.bfloat16),
            pltpu.VMEM((4, RING * COLS, COLS), jnp.bfloat16),
            pltpu.VMEM((CHUNKS, 2, CHUNK, COLS), jnp.float32),
            pltpu.VMEM((CHUNKS, 2, CHUNK, COLS), jnp.float32),
            pltpu.VMEM((STEPS, 2, CHUNK, COLS), jnp.float32),
            pltpu.VMEM((CHUNKS, CHUNK, COLS), jnp.bfloat16),
            pltpu.VMEM((STEPS, CHUNK, COLS), jnp.bfloat16),
        ]
        + [dma((STEPS,))] * 12
        + [dma, dma, dma((4,)), dma((4,)), dma((6,)), dma((10,)), dma((16,))],
        compiler_params=pltpu.CompilerParams(
            collective_id=0, has_side_effects=True, vmem_limit_bytes=56 * 1024 * 1024
        ),
        cost_estimate=pl.CostEstimate(
            flops=3 * 2 * ROWS * 1024 * 1024,
            bytes_accessed=4 * 1024 * 1024,
            transcendentals=0,
        ),
    )(tile_sizes, screen_ov.T, screen_vv, coupling, denominators, integrals)


def solution(mesh):
    in_specs = (P("blk", "bcast"), P("blk", "bcast"), P("bcast", "blk"), P(), P(), P())
    out_specs = P("blk", "bcast")
    return jax.shard_map(local, mesh=mesh, in_specs=in_specs, out_specs=out_specs, check_vma=False)
```

```python
import jax
import jax.numpy as jnp
from jax import lax
from jax.experimental import pallas as pl
from jax.experimental.pallas import tpu as pltpu
from jax.sharding import PartitionSpec as P

TILE = 128
ROW_TILE = 128
ITERS = 3
MESH = pl.DeviceIdType.MESH

ROWS = 1024
COLS = 256
CHUNK = 128
CHUNKS = ROWS // CHUNK
SPLIT = ROW_TILE // CHUNK
STEPS = ITERS * CHUNKS
HALF = CHUNK // 2
FINAL = 4
SECOND = 2
FORWARD = 6
RING = 4


def device(x, y, z, core):
    x, y, z, core = x % 4, y % 4, z % 4, core % 2
    return (x * 2 + z % 2, ((z // 2) * 4 + y) * 2 + core)


def kernel(
    sizes_hbm,
    ov_hbm,
    vv_hbm,
    coupling_hbm,
    den_hbm,
    integrals_hbm,
    out_hbm,
    sizes_ref,
    ov_ref,
    vv_ref,
    coupling_ref,
    den_ref,
    integrals_ref,
    loaded,
    result,
    stored,
    weight,
    amp,
    swap,
    unit,
    ring,
    table,
    sib_out,
    own,
    sib_in,
    z_out,
    z_in,
    up_send,
    down_send,
    up_recv,
    down_recv,
    fup_send,
    fdown_send,
    fup_recv,
    fdown_recv,
    sib_send,
    sib_recv,
    z_send,
    z_recv,
    swap_send,
    swap_recv,
    ring_send,
    ring_recv,
    o_send,
    s_send,
    t_recv,
):
    blk = lax.axis_index("blk")
    bcast = lax.axis_index("bcast")
    x, zl = blk // 2, blk % 2
    zh, y, core = bcast // 8, (bcast // 2) % 4, bcast % 2
    z = zh * 2 + zl
    up = device(x, y + 1, z, core)
    down = device(x, y + 3, z, core)
    sibling = device(x, y, z, core + 1)
    across = device(x, y, z + 2, core)
    x_pair, x_out = x + 1 - 2 * (x % 2), x - 1 + 2 * (x % 2)
    z_mate, z_next = z + 1 - 2 * zl, z - 1 + 2 * zl
    pair_x = device(x_pair, y, z, core)
    out_x = device(x_out + 4, y, z, core)
    pair_z = device(x, y, z_mate, core)
    out_z = device(x, y, z_next + 4, core)
    right = device(x + 1, y, z, core)
    left = device(x + 3, y, z, core)
    inside = (x // 2) == zh
    outside = jnp.logical_not(inside)

    loads = [
        pltpu.make_async_copy(src, dst, loaded.at[n])
        for n, (src, dst) in enumerate(
            (
                (vv_hbm, vv_ref),
                (integrals_hbm, integrals_ref),
                (sizes_hbm, sizes_ref),
                (ov_hbm, ov_ref),
                (coupling_hbm, coupling_ref),
                (den_hbm, den_ref),
            )
        )
    ]
    barrier = pltpu.get_barrier_semaphore()
    for dev in (up, down, sibling, across, pair_x, out_x, pair_z, out_z):
        pl.semaphore_signal(barrier, inc=1, device_id=dev, device_id_type=MESH)
    for load in loads:
        load.start()

    def screened(h, ref):
        for j in range(2):
            for i in range(2):
                keep = vv_ref[bcast * 2 + i, blk * 4 + h * 2 + j].astype(jnp.float32)
                at = pl.ds(pl.multiple_of((h * 2 + j) * TILE, TILE), TILE)
                part = integrals_ref[pl.ds(i * TILE, TILE), at].astype(jnp.float32)
                ref[pl.ds(j * TILE, TILE), pl.ds(i * TILE, TILE)] = jnp.transpose(
                    part * keep
                ).astype(jnp.bfloat16)

    loads[0].wait()
    loads[1].wait()
    screened(1 - core, swap)
    screened(core, ring.at[x])

    def rows_of(k):
        return pl.ds(pl.multiple_of(k * CHUNK, CHUNK), CHUNK)

    def first_amplitudes(k):
        lane = lax.broadcasted_iota(jnp.int32, (CHUNK, COLS), 1)
        size0, size1 = sizes_ref[bcast * 2], sizes_ref[bcast * 2 + 1]
        ov0 = ov_ref[bcast * 2, blk * 8 + k // SPLIT]
        ov1 = ov_ref[bcast * 2 + 1, blk * 8 + k // SPLIT]
        live0 = jnp.where(lane < size0, ov0, 0)
        live1 = jnp.where(lane - TILE < size1, ov1, 0)
        keep = jnp.where(lane < TILE, live0, live1).astype(jnp.float32)
        w = keep / den_ref[rows_of(k), :]
        weight[rows_of(k), :] = w
        amp[0, y, rows_of(k), :] = (coupling_ref[rows_of(k), :] * w).astype(jnp.bfloat16)

    def part_of(t, owner, k, offset, length):
        start = pl.multiple_of(k * CHUNK + offset, HALF)
        return amp.at[t, owner, pl.ds(start, length), :]

    def remote(ref, target, send, recv):
        return pltpu.make_async_remote_copy(
            src_ref=ref, dst_ref=ref, send_sem=send, recv_sem=recv,
            device_id=target, device_id_type=MESH,
        )

    def send_up(s):
        ref = part_of(s // CHUNKS, y, s % CHUNKS, 0, CHUNK)
        return remote(ref, up, up_send.at[s], up_recv.at[s])

    def send_down(s):
        ref = part_of(s // CHUNKS, y, s % CHUNKS, 0, CHUNK)
        return remote(ref, down, down_send.at[s], down_recv.at[s])

    below, above, far = (y + 3) % RING, (y + 1) % RING, (y + 2) % RING

    def from_below(s):
        ref = part_of(s // CHUNKS, below, s % CHUNKS, 0, CHUNK)
        return remote(ref, up, up_send.at[s], up_recv.at[s])

    def from_above(s):
        ref = part_of(s // CHUNKS, above, s % CHUNKS, 0, CHUNK)
        return remote(ref, down, down_send.at[s], down_recv.at[s])

    def pass_up(s):
        ref = part_of(s // CHUNKS, below, s % CHUNKS, 0, HALF)
        return remote(ref, up, fup_send.at[s], fup_recv.at[s])

    def pass_down(s):
        ref = part_of(s // CHUNKS, above, s % CHUNKS, HALF, HALF)
        return remote(ref, down, fdown_send.at[s], fdown_recv.at[s])

    def far_from_below(s):
        ref = part_of(s // CHUNKS, far, s % CHUNKS, 0, HALF)
        return remote(ref, up, fup_send.at[s], fup_recv.at[s])

    def far_from_above(s):
        ref = part_of(s // CHUNKS, far, s % CHUNKS, HALF, HALF)
        return remote(ref, down, fdown_send.at[s], fdown_recv.at[s])

    def to_sibling(s, part):
        return pltpu.make_async_remote_copy(
            src_ref=sib_out.at[s % CHUNKS, part], dst_ref=sib_in.at[s, part],
            send_sem=sib_send.at[s * 2 + part], recv_sem=sib_recv.at[s * 2 + part],
            device_id=sibling, device_id_type=MESH,
        )

    def to_across(s):
        return pltpu.make_async_remote_copy(
            src_ref=z_out.at[s % CHUNKS], dst_ref=z_in.at[s],
            send_sem=z_send.at[s], recv_sem=z_recv.at[s],
            device_id=across, device_id_type=MESH,
        )

    def start_ring(s):
        send_up(s).start()
        send_down(s).start()

    def forward(s):
        from_below(s).wait_recv()
        pass_up(s).start()
        from_above(s).wait_recv()
        pass_down(s).start()

    def gathered(s):
        far_from_below(s).wait_recv()
        far_from_above(s).wait_recv()

    def product(s, part):
        t, k = s // CHUNKS, s % CHUNKS
        block = 2 * (zh if part else 1 - zh)
        lhs = jnp.concatenate([amp[t, o, rows_of(k), :] for o in range(RING)], axis=1)
        sib_out[k, part] = jnp.dot(
            lhs, table[block + 1 - core], preferred_element_type=jnp.float32
        )
        to_sibling(s, part).start()
        own[k, part] = jnp.dot(
            lhs, table[block + core], preferred_element_type=jnp.float32
        )

    def store(k):
        rows = rows_of(k)
        return pltpu.make_async_copy(
            result.at[rows, :], out_hbm.at[rows, :], stored.at[k]
        )

    def reduce_core(s):
        k = s % CHUNKS
        to_sibling(s, 0).wait()
        z_out[k] = (own[k, 0] + sib_in[s, 0]).astype(jnp.bfloat16)
        to_across(s).start()

    def finish(s):
        t, k = s // CHUNKS, s % CHUNKS
        to_sibling(s, 1).wait()
        to_across(s).wait()
        ladder = own[k, 1] + sib_in[s, 1] + z_in[s].astype(jnp.float32)
        value = (coupling_ref[rows_of(k), :] + ladder) * weight[rows_of(k), :]

        @pl.when(t < ITERS - 1)
        def _():
            amp[t + 1, y, rows_of(k), :] = value.astype(jnp.bfloat16)
            start_ring(s + CHUNKS)

        @pl.when(t == ITERS - 1)
        def _():
            result[rows_of(k), :] = value
            store(k).start()

        send_up(s).wait_send()
        send_down(s).wait_send()
        pass_up(s).wait_send()
        pass_down(s).wait_send()

    def slot_of(first_core, zh_of, parity, zl_of):
        return (zh_of * 2 + first_core) * 4 + parity * 2 + zl_of

    def at_slot(slot):
        start = pl.multiple_of((slot % 4) * COLS, COLS)
        return table.at[slot // 4, pl.ds(start, COLS), :]

    def unit_copy(src, slot, send, target):
        return pltpu.make_async_remote_copy(
            src_ref=src, dst_ref=at_slot(slot), send_sem=send, recv_sem=t_recv.at[slot],
            device_id=target, device_id_type=MESH,
        )

    def arrived(slot):
        unit_copy(at_slot(slot), slot, swap_send, sibling).wait_recv()

    to_swap = pltpu.make_async_remote_copy(
        src_ref=swap, dst_ref=unit, send_sem=swap_send, recv_sem=swap_recv,
        device_id=sibling, device_id_type=MESH,
    )
    parity = x % 2

    def ring_part(owner, half):
        owner = (owner + 4) % 4
        if half is None:
            return ring.at[owner]
        return ring.at[owner, pl.ds(half * TILE, TILE), :]

    def ring_copy(owner, half, n, target):
        ref = ring_part(owner, half)
        return remote(ref, target, ring_send.at[n], ring_recv.at[n])

    def o_slot(owner):
        return slot_of(core, zh, owner % 2, zl)

    def over_z(n):
        owner = (x + (0, 3, 1, 2)[n]) % 4
        target = tuple(
            jnp.where(owner // 2 == zh, a, b) for a, b in zip(pair_z, out_z)
        )
        return unit_copy(ring.at[owner], o_slot(owner), o_send.at[n], target)

    def o_pass(n):
        slot = slot_of(core, 1 - zh, n, 1 - zl)
        return unit_copy(at_slot(slot), slot, o_send.at[4 + n], pair_z)

    s_slots = [
        lambda par, a=a, b=b: slot_of(1 - core, a, par, b)
        for a, b in ((zh, zl), (zh, 1 - zl), (1 - zh, 1 - zl), (1 - zh, zl))
    ]
    first_target = tuple(jnp.where(inside, a, b) for a, b in zip(pair_z, out_z))
    s_first = unit_copy(unit, s_slots[0](parity), s_send.at[0], first_target)
    s_pass = unit_copy(
        at_slot(s_slots[2](parity)), s_slots[2](parity), s_send.at[1], pair_z
    )

    def s_inside(n, k):
        slot = s_slots[n](parity)
        src = unit if n == 0 else at_slot(slot)
        return unit_copy(src, slot, s_send.at[2 + 2 * n + k], (pair_x, out_x)[k])

    def s_outside(n):
        slot = s_slots[n](1 - parity)
        return unit_copy(at_slot(slot), slot, s_send.at[2 + 2 * n], pair_x)

    def s_start(n):
        s_inside(n, 1).start()
        s_inside(n, 0).start()

    def s_relay(n):
        arrived(s_slots[n](1 - parity))
        s_outside(n).start()

    def forwards(eighth):
        @pl.loop(eighth * (CHUNKS // 8), (eighth + 1) * (CHUNKS // 8))
        def _(k):
            forward(k)

    for load in loads[2:]:
        load.wait()

    @pl.loop(0, CHUNKS)
    def _(k):
        first_amplitudes(k)

    pl.semaphore_wait(barrier, 8)
    to_swap.start()
    ring_copy(x, None, 0, right).start()
    ring_copy(x, None, 1, left).start()
    over_z(0).start()
    start_ring(0)

    to_swap.wait_recv()
    s_first.start()

    @pl.when(inside)
    def _():
        s_start(0)
        table[(zh * 2 + 1 - core), pl.ds(pl.multiple_of((parity * 2 + zl) * COLS, COLS), COLS), :] = unit[...]

    @pl.loop(1, CHUNKS // 2)
    def _(k):
        start_ring(k)

    ring_copy(x + 3, None, 0, right).wait_recv()
    ring_copy(x + 3, 0, 2, right).start()
    over_z(1).start()
    ring_copy(x + 1, None, 1, left).wait_recv()
    ring_copy(x + 1, 1, 3, left).start()
    over_z(2).start()

    @pl.loop(CHUNKS // 2, CHUNKS)
    def _(k):
        start_ring(k)

    forwards(0)

    @pl.when(inside)
    def _():
        arrived(s_slots[1](parity))
        s_start(1)
        arrived(s_slots[2](parity))
        s_pass.start()
        s_start(2)

    @pl.when(outside)
    def _():
        s_relay(0)

    ring_copy(x + 2, 0, 2, right).wait_recv()
    ring_copy(x + 2, 1, 3, left).wait_recv()
    over_z(3).start()
    for p in range(2):
        owner = 2 * zh + p
        table[zh * 2 + core, pl.ds(pl.multiple_of((p * 2 + zl) * COLS, COLS), COLS), :] = ring[owner]
    forwards(1)
    forwards(2)
    pl.when(outside)(lambda: s_relay(1))
    forwards(3)

    @pl.when(inside)
    def _():
        arrived(s_slots[3](parity))
        s_start(3)

    pl.when(outside)(lambda: s_relay(2))
    for n in range(2):
        arrived(slot_of(core, 1 - zh, n, 1 - zl))
        o_pass(n).start()
        forwards(4 + n)
    pl.when(outside)(lambda: s_relay(3))
    forwards(6)
    forwards(7)
    from_pair = jnp.where(inside, 1 - parity, parity)
    for n in range(2):
        arrived(slot_of(core, 1 - zh, n, zl))
        arrived(s_slots[2 + n](from_pair))
    gathered(0)
    product(0, 0)
    gathered(1)
    product(1, 0)
    reduce_core(0)
    for n in range(2):
        arrived(slot_of(core, zh, n, 1 - zl))
        arrived(s_slots[n](from_pair))

    def tick_of(tick, lag):
        return jnp.logical_and(tick >= lag, tick < STEPS + lag)

    @pl.loop(2, STEPS + FINAL)
    def _(tick):
        @pl.when(tick_of(tick, FINAL))
        def _():
            finish(tick - FINAL)

        @pl.when(jnp.logical_and(tick >= FORWARD, tick < STEPS - CHUNKS + FORWARD))
        def _():
            forward(tick - FORWARD + CHUNKS)

        @pl.when(tick_of(tick, 1))
        def _():
            reduce_core(tick - 1)

        @pl.when(tick < STEPS)
        def _():
            gathered(tick)
            product(tick, 0)

        @pl.when(tick_of(tick, SECOND))
        def _():
            product(tick - SECOND, 1)

    for k in range(CHUNKS):
        store(k).wait()
    to_swap.wait_send()
    for n, (owner, half) in enumerate(((x, None), (x, None), (x + 3, 0), (x + 1, 1))):
        ring_copy(owner, half, n, right).wait_send()
    for n in range(4):
        over_z(n).wait_send()
    o_pass(0).wait_send()
    o_pass(1).wait_send()
    s_first.wait_send()

    @pl.when(inside)
    def _():
        s_pass.wait_send()
        for n in range(4):
            for k in range(2):
                s_inside(n, k).wait_send()

    @pl.when(outside)
    def _():
        for n in range(4):
            s_outside(n).wait_send()


def local(coupling, denominators, integrals, tile_sizes, screen_ov, screen_vv):
    dma = pltpu.SemaphoreType.DMA
    anywhere = pl.BlockSpec(memory_space=pl.ANY)
    return pl.pallas_call(
        kernel,
        out_shape=jax.ShapeDtypeStruct((ROWS, COLS), jnp.float32),
        in_specs=[anywhere] * 6,
        out_specs=anywhere,
        scratch_shapes=[
            pltpu.SMEM((32,), jnp.int32),
            pltpu.SMEM((32, 64), jnp.int32),
            pltpu.SMEM((32, 32), jnp.int32),
            pltpu.VMEM((ROWS, COLS), jnp.float32),
            pltpu.VMEM((ROWS, COLS), jnp.float32),
            pltpu.VMEM((COLS, 2 * COLS), jnp.bfloat16),
            dma((6,)),
            pltpu.VMEM((ROWS, COLS), jnp.float32),
            dma((CHUNKS,)),
            pltpu.VMEM((ROWS, COLS), jnp.float32),
            pltpu.VMEM((ITERS, RING, ROWS, COLS), jnp.bfloat16),
            pltpu.VMEM((COLS, COLS), jnp.bfloat16),
            pltpu.VMEM((COLS, COLS), jnp.bfloat16),
            pltpu.VMEM((4, COLS, COLS), jnp.bfloat16),
            pltpu.VMEM((4, RING * COLS, COLS), jnp.bfloat16),
            pltpu.VMEM((CHUNKS, 2, CHUNK, COLS), jnp.float32),
            pltpu.VMEM((CHUNKS, 2, CHUNK, COLS), jnp.float32),
            pltpu.VMEM((STEPS, 2, CHUNK, COLS), jnp.float32),
            pltpu.VMEM((CHUNKS, CHUNK, COLS), jnp.bfloat16),
            pltpu.VMEM((STEPS, CHUNK, COLS), jnp.bfloat16),
        ]
        + [dma((STEPS,))] * 8
        + [dma((2 * STEPS,))] * 2
        + [dma((STEPS,))] * 2
        + [dma, dma, dma((4,)), dma((4,)), dma((6,)), dma((10,)), dma((16,))],
        compiler_params=pltpu.CompilerParams(
            collective_id=0, has_side_effects=True, vmem_limit_bytes=56 * 1024 * 1024
        ),
        cost_estimate=pl.CostEstimate(
            flops=3 * 2 * ROWS * 1024 * 1024,
            bytes_accessed=4 * 1024 * 1024,
            transcendentals=0,
        ),
    )(tile_sizes, screen_ov.T, screen_vv, coupling, denominators, integrals)


def solution(mesh):
    in_specs = (P("blk", "bcast"), P("blk", "bcast"), P("bcast", "blk"), P(), P(), P())
    out_specs = P("blk", "bcast")
    return jax.shard_map(local, mesh=mesh, in_specs=in_specs, out_specs=out_specs, check_vma=False)
```

```python
import jax
import jax.numpy as jnp
from jax import lax
from jax.experimental import pallas as pl
from jax.experimental.pallas import tpu as pltpu
from jax.sharding import PartitionSpec as P

TILE = 128
ROW_TILE = 128
ITERS = 3
MESH = pl.DeviceIdType.MESH

ROWS = 1024
COLS = 256
CHUNK = 128
CHUNKS = ROWS // CHUNK
SPLIT = ROW_TILE // CHUNK
STEPS = ITERS * CHUNKS
HALF = CHUNK // 2
SCALE_ROWS = 16
FINAL = 4
SECOND = 2
FORWARD = 6
RING = 4


def device(x, y, z, core):
    x, y, z, core = x % 4, y % 4, z % 4, core % 2
    return (x * 2 + z % 2, ((z // 2) * 4 + y) * 2 + core)


def kernel(
    sizes_hbm,
    ov_hbm,
    vv_hbm,
    coupling_hbm,
    den_hbm,
    integrals_hbm,
    out_hbm,
    sizes_ref,
    ov_ref,
    vv_ref,
    coupling_ref,
    den_ref,
    integrals_ref,
    loaded,
    result,
    stored,
    weight,
    amp,
    swap,
    unit,
    ring,
    table,
    sib_out,
    own,
    sib_in,
    z_out,
    z_in,
    up_send,
    down_send,
    up_recv,
    down_recv,
    fup_send,
    fdown_send,
    fup_recv,
    fdown_recv,
    sib_send,
    sib_recv,
    z_send,
    z_recv,
    swap_send,
    swap_recv,
    ring_send,
    ring_recv,
    o_send,
    s_send,
    t_recv,
):
    blk = lax.axis_index("blk")
    bcast = lax.axis_index("bcast")
    x, zl = blk // 2, blk % 2
    zh, y, core = bcast // 8, (bcast // 2) % 4, bcast % 2
    z = zh * 2 + zl
    up = device(x, y + 1, z, core)
    down = device(x, y + 3, z, core)
    sibling = device(x, y, z, core + 1)
    across = device(x, y, z + 2, core)
    x_pair, x_out = x + 1 - 2 * (x % 2), x - 1 + 2 * (x % 2)
    z_mate, z_next = z + 1 - 2 * zl, z - 1 + 2 * zl
    pair_x = device(x_pair, y, z, core)
    out_x = device(x_out + 4, y, z, core)
    pair_z = device(x, y, z_mate, core)
    out_z = device(x, y, z_next + 4, core)
    right = device(x + 1, y, z, core)
    left = device(x + 3, y, z, core)
    inside = (x // 2) == zh
    outside = jnp.logical_not(inside)

    loads = [
        pltpu.make_async_copy(src, dst, loaded.at[n])
        for n, (src, dst) in enumerate(
            (
                (vv_hbm, vv_ref),
                (integrals_hbm, integrals_ref),
                (sizes_hbm, sizes_ref),
                (ov_hbm, ov_ref),
                (coupling_hbm, coupling_ref),
                (den_hbm, den_ref),
            )
        )
    ]
    barrier = pltpu.get_barrier_semaphore()
    for dev in (up, down, sibling, across, pair_x, out_x, pair_z, out_z):
        pl.semaphore_signal(barrier, inc=1, device_id=dev, device_id_type=MESH)
    for load in loads:
        load.start()

    def screened(h, ref):
        for j in range(2):
            for i in range(2):
                keep = vv_ref[bcast * 2 + i, blk * 4 + h * 2 + j].astype(jnp.float32)
                at = pl.ds(pl.multiple_of((h * 2 + j) * TILE, TILE), TILE)
                part = integrals_ref[pl.ds(i * TILE, TILE), at].astype(jnp.float32)
                ref[pl.ds(j * TILE, TILE), pl.ds(i * TILE, TILE)] = jnp.transpose(
                    part * keep
                ).astype(jnp.bfloat16)

    loads[0].wait()
    loads[1].wait()
    screened(1 - core, swap)
    screened(core, ring.at[x])

    def rows_of(k):
        return pl.ds(pl.multiple_of(k * CHUNK, CHUNK), CHUNK)

    def first_amplitudes(k):
        lane = lax.broadcasted_iota(jnp.int32, (CHUNK, COLS), 1)
        size0, size1 = sizes_ref[bcast * 2], sizes_ref[bcast * 2 + 1]
        ov0 = ov_ref[bcast * 2, blk * 8 + k // SPLIT]
        ov1 = ov_ref[bcast * 2 + 1, blk * 8 + k // SPLIT]
        live0 = jnp.where(lane < size0, ov0, 0)
        live1 = jnp.where(lane - TILE < size1, ov1, 0)
        keep = jnp.where(lane < TILE, live0, live1).astype(jnp.float32)
        w = keep / den_ref[rows_of(k), :]
        weight[rows_of(k), :] = w
        amp[0, y, rows_of(k), :] = (coupling_ref[rows_of(k), :] * w).astype(jnp.bfloat16)

    def part_of(t, owner, k, offset, length):
        start = pl.multiple_of(k * CHUNK + offset, HALF)
        return amp.at[t, owner, pl.ds(start, length), :]

    def remote(ref, target, send, recv):
        return pltpu.make_async_remote_copy(
            src_ref=ref, dst_ref=ref, send_sem=send, recv_sem=recv,
            device_id=target, device_id_type=MESH,
        )

    def send_up(s):
        ref = part_of(s // CHUNKS, y, s % CHUNKS, 0, CHUNK)
        return remote(ref, up, up_send.at[s], up_recv.at[s])

    def send_down(s):
        ref = part_of(s // CHUNKS, y, s % CHUNKS, 0, CHUNK)
        return remote(ref, down, down_send.at[s], down_recv.at[s])

    below, above, far = (y + 3) % RING, (y + 1) % RING, (y + 2) % RING

    def from_below(s):
        ref = part_of(s // CHUNKS, below, s % CHUNKS, 0, CHUNK)
        return remote(ref, up, up_send.at[s], up_recv.at[s])

    def from_above(s):
        ref = part_of(s // CHUNKS, above, s % CHUNKS, 0, CHUNK)
        return remote(ref, down, down_send.at[s], down_recv.at[s])

    def pass_up(s):
        ref = part_of(s // CHUNKS, below, s % CHUNKS, 0, HALF)
        return remote(ref, up, fup_send.at[s], fup_recv.at[s])

    def pass_down(s):
        ref = part_of(s // CHUNKS, above, s % CHUNKS, HALF, HALF)
        return remote(ref, down, fdown_send.at[s], fdown_recv.at[s])

    def far_from_below(s):
        ref = part_of(s // CHUNKS, far, s % CHUNKS, 0, HALF)
        return remote(ref, up, fup_send.at[s], fup_recv.at[s])

    def far_from_above(s):
        ref = part_of(s // CHUNKS, far, s % CHUNKS, HALF, HALF)
        return remote(ref, down, fdown_send.at[s], fdown_recv.at[s])

    def to_sibling(s, part):
        return pltpu.make_async_remote_copy(
            src_ref=sib_out.at[s % CHUNKS, part], dst_ref=sib_in.at[s, part],
            send_sem=sib_send.at[s * 2 + part], recv_sem=sib_recv.at[s * 2 + part],
            device_id=sibling, device_id_type=MESH,
        )

    def to_across(s):
        return pltpu.make_async_remote_copy(
            src_ref=z_out.at[s % CHUNKS], dst_ref=z_in.at[s],
            send_sem=z_send.at[s], recv_sem=z_recv.at[s],
            device_id=across, device_id_type=MESH,
        )

    def start_ring(s):
        send_up(s).start()
        send_down(s).start()

    def forward(s):
        from_below(s).wait_recv()
        pass_up(s).start()
        from_above(s).wait_recv()
        pass_down(s).start()

    def gathered(s):
        far_from_below(s).wait_recv()
        far_from_above(s).wait_recv()

    def product(s, part):
        t, k = s // CHUNKS, s % CHUNKS
        block = 2 * (zh if part else 1 - zh)
        lhs = jnp.concatenate([amp[t, o, rows_of(k), :] for o in range(RING)], axis=1)
        sib_out[k, part] = jnp.dot(
            lhs, table[block + 1 - core], preferred_element_type=jnp.float32
        )
        to_sibling(s, part).start()
        own[k, part] = jnp.dot(
            lhs, table[block + core], preferred_element_type=jnp.float32
        )

    def store(k):
        rows = rows_of(k)
        return pltpu.make_async_copy(
            result.at[rows, :], out_hbm.at[rows, :], stored.at[k]
        )

    def reduce_core(s):
        k = s % CHUNKS
        to_sibling(s, 0).wait()
        partial = own[k, 0] + sib_in[s, 0]
        most = jnp.max(jnp.abs(partial), axis=0, keepdims=True)
        log = jnp.floor(jnp.log2(jnp.maximum(most, 1e-30)) * 128.0) + 2.0
        coded = jnp.round(partial * (32766.0 * jnp.exp2(log * (-1.0 / 128.0))))
        z_out[k, pl.ds(0, CHUNK), :] = coded.astype(jnp.int32).astype(jnp.int16)
        logs = jnp.broadcast_to(log.astype(jnp.int32), (SCALE_ROWS, COLS))
        z_out[k, pl.ds(CHUNK, SCALE_ROWS), :] = logs.astype(jnp.int16)
        to_across(s).start()

    def finish(s):
        t, k = s // CHUNKS, s % CHUNKS
        to_sibling(s, 1).wait()
        to_across(s).wait()
        logs = z_in[s, pl.ds(CHUNK, SCALE_ROWS), :].astype(jnp.int32).astype(jnp.float32)
        scale = jnp.exp2(logs * (1.0 / 128.0))[:1] * (1.0 / 32766.0)
        coded = z_in[s, pl.ds(0, CHUNK), :].astype(jnp.int32).astype(jnp.float32)
        ladder = own[k, 1] + sib_in[s, 1] + coded * scale
        value = (coupling_ref[rows_of(k), :] + ladder) * weight[rows_of(k), :]

        @pl.when(t < ITERS - 1)
        def _():
            amp[t + 1, y, rows_of(k), :] = value.astype(jnp.bfloat16)
            start_ring(s + CHUNKS)

        @pl.when(t == ITERS - 1)
        def _():
            result[rows_of(k), :] = value
            store(k).start()

        send_up(s).wait_send()
        send_down(s).wait_send()
        pass_up(s).wait_send()
        pass_down(s).wait_send()

    def slot_of(first_core, zh_of, parity, zl_of):
        return (zh_of * 2 + first_core) * 4 + parity * 2 + zl_of

    def at_slot(slot):
        start = pl.multiple_of((slot % 4) * COLS, COLS)
        return table.at[slot // 4, pl.ds(start, COLS), :]

    def unit_copy(src, slot, send, target):
        return pltpu.make_async_remote_copy(
            src_ref=src, dst_ref=at_slot(slot), send_sem=send, recv_sem=t_recv.at[slot],
            device_id=target, device_id_type=MESH,
        )

    def arrived(slot):
        unit_copy(at_slot(slot), slot, swap_send, sibling).wait_recv()

    to_swap = pltpu.make_async_remote_copy(
        src_ref=swap, dst_ref=unit, send_sem=swap_send, recv_sem=swap_recv,
        device_id=sibling, device_id_type=MESH,
    )
    parity = x % 2

    def ring_part(owner, half):
        owner = (owner + 4) % 4
        if half is None:
            return ring.at[owner]
        return ring.at[owner, pl.ds(half * TILE, TILE), :]

    def ring_copy(owner, half, n, target):
        ref = ring_part(owner, half)
        return remote(ref, target, ring_send.at[n], ring_recv.at[n])

    def o_slot(owner):
        return slot_of(core, zh, owner % 2, zl)

    def over_z(n):
        owner = (x + (0, 3, 1, 2)[n]) % 4
        target = tuple(
            jnp.where(owner // 2 == zh, a, b) for a, b in zip(pair_z, out_z)
        )
        return unit_copy(ring.at[owner], o_slot(owner), o_send.at[n], target)

    def o_pass(n):
        slot = slot_of(core, 1 - zh, n, 1 - zl)
        return unit_copy(at_slot(slot), slot, o_send.at[4 + n], pair_z)

    s_slots = [
        lambda par, a=a, b=b: slot_of(1 - core, a, par, b)
        for a, b in ((zh, zl), (zh, 1 - zl), (1 - zh, 1 - zl), (1 - zh, zl))
    ]
    first_target = tuple(jnp.where(inside, a, b) for a, b in zip(pair_z, out_z))
    s_first = unit_copy(unit, s_slots[0](parity), s_send.at[0], first_target)
    s_pass = unit_copy(
        at_slot(s_slots[2](parity)), s_slots[2](parity), s_send.at[1], pair_z
    )

    def s_inside(n, k):
        slot = s_slots[n](parity)
        src = unit if n == 0 else at_slot(slot)
        return unit_copy(src, slot, s_send.at[2 + 2 * n + k], (pair_x, out_x)[k])

    def s_outside(n):
        slot = s_slots[n](1 - parity)
        return unit_copy(at_slot(slot), slot, s_send.at[2 + 2 * n], pair_x)

    def s_start(n):
        s_inside(n, 1).start()
        s_inside(n, 0).start()

    def s_relay(n):
        arrived(s_slots[n](1 - parity))
        s_outside(n).start()

    def forwards(eighth):
        @pl.loop(eighth * (CHUNKS // 8), (eighth + 1) * (CHUNKS // 8))
        def _(k):
            forward(k)

    for load in loads[2:]:
        load.wait()

    @pl.loop(0, CHUNKS)
    def _(k):
        first_amplitudes(k)

    pl.semaphore_wait(barrier, 8)
    to_swap.start()
    ring_copy(x, None, 0, right).start()
    ring_copy(x, None, 1, left).start()
    over_z(0).start()
    start_ring(0)

    to_swap.wait_recv()
    s_first.start()

    @pl.when(inside)
    def _():
        s_start(0)
        table[(zh * 2 + 1 - core), pl.ds(pl.multiple_of((parity * 2 + zl) * COLS, COLS), COLS), :] = unit[...]

    @pl.loop(1, CHUNKS // 2)
    def _(k):
        start_ring(k)

    ring_copy(x + 3, None, 0, right).wait_recv()
    ring_copy(x + 3, 0, 2, right).start()
    over_z(1).start()
    ring_copy(x + 1, None, 1, left).wait_recv()
    ring_copy(x + 1, 1, 3, left).start()
    over_z(2).start()

    @pl.loop(CHUNKS // 2, CHUNKS)
    def _(k):
        start_ring(k)

    forwards(0)

    @pl.when(inside)
    def _():
        arrived(s_slots[1](parity))
        s_start(1)
        arrived(s_slots[2](parity))
        s_pass.start()
        s_start(2)

    @pl.when(outside)
    def _():
        s_relay(0)

    ring_copy(x + 2, 0, 2, right).wait_recv()
    ring_copy(x + 2, 1, 3, left).wait_recv()
    over_z(3).start()
    for p in range(2):
        owner = 2 * zh + p
        table[zh * 2 + core, pl.ds(pl.multiple_of((p * 2 + zl) * COLS, COLS), COLS), :] = ring[owner]
    forwards(1)
    forwards(2)
    pl.when(outside)(lambda: s_relay(1))
    forwards(3)

    @pl.when(inside)
    def _():
        arrived(s_slots[3](parity))
        s_start(3)

    pl.when(outside)(lambda: s_relay(2))
    for n in range(2):
        arrived(slot_of(core, 1 - zh, n, 1 - zl))
        o_pass(n).start()
        forwards(4 + n)
    pl.when(outside)(lambda: s_relay(3))
    forwards(6)
    forwards(7)
    from_pair = jnp.where(inside, 1 - parity, parity)
    for n in range(2):
        arrived(slot_of(core, 1 - zh, n, zl))
        arrived(s_slots[2 + n](from_pair))
    gathered(0)
    product(0, 0)
    gathered(1)
    product(1, 0)
    reduce_core(0)
    for n in range(2):
        arrived(slot_of(core, zh, n, 1 - zl))
        arrived(s_slots[n](from_pair))

    def tick_of(tick, lag):
        return jnp.logical_and(tick >= lag, tick < STEPS + lag)

    @pl.loop(2, STEPS + FINAL)
    def _(tick):
        @pl.when(tick_of(tick, FINAL))
        def _():
            finish(tick - FINAL)

        @pl.when(jnp.logical_and(tick >= FORWARD, tick < STEPS - CHUNKS + FORWARD))
        def _():
            forward(tick - FORWARD + CHUNKS)

        @pl.when(tick_of(tick, 1))
        def _():
            reduce_core(tick - 1)

        @pl.when(tick < STEPS)
        def _():
            gathered(tick)
            product(tick, 0)

        @pl.when(tick_of(tick, SECOND))
        def _():
            product(tick - SECOND, 1)

    for k in range(CHUNKS):
        store(k).wait()
    to_swap.wait_send()
    for n, (owner, half) in enumerate(((x, None), (x, None), (x + 3, 0), (x + 1, 1))):
        ring_copy(owner, half, n, right).wait_send()
    for n in range(4):
        over_z(n).wait_send()
    o_pass(0).wait_send()
    o_pass(1).wait_send()
    s_first.wait_send()

    @pl.when(inside)
    def _():
        s_pass.wait_send()
        for n in range(4):
            for k in range(2):
                s_inside(n, k).wait_send()

    @pl.when(outside)
    def _():
        for n in range(4):
            s_outside(n).wait_send()


def local(coupling, denominators, integrals, tile_sizes, screen_ov, screen_vv):
    dma = pltpu.SemaphoreType.DMA
    anywhere = pl.BlockSpec(memory_space=pl.ANY)
    return pl.pallas_call(
        kernel,
        out_shape=jax.ShapeDtypeStruct((ROWS, COLS), jnp.float32),
        in_specs=[anywhere] * 6,
        out_specs=anywhere,
        scratch_shapes=[
            pltpu.SMEM((32,), jnp.int32),
            pltpu.SMEM((32, 64), jnp.int32),
            pltpu.SMEM((32, 32), jnp.int32),
            pltpu.VMEM((ROWS, COLS), jnp.float32),
            pltpu.VMEM((ROWS, COLS), jnp.float32),
            pltpu.VMEM((COLS, 2 * COLS), jnp.bfloat16),
            dma((6,)),
            pltpu.VMEM((ROWS, COLS), jnp.float32),
            dma((CHUNKS,)),
            pltpu.VMEM((ROWS, COLS), jnp.float32),
            pltpu.VMEM((ITERS, RING, ROWS, COLS), jnp.bfloat16),
            pltpu.VMEM((COLS, COLS), jnp.bfloat16),
            pltpu.VMEM((COLS, COLS), jnp.bfloat16),
            pltpu.VMEM((4, COLS, COLS), jnp.bfloat16),
            pltpu.VMEM((4, RING * COLS, COLS), jnp.bfloat16),
            pltpu.VMEM((CHUNKS, 2, CHUNK, COLS), jnp.float32),
            pltpu.VMEM((CHUNKS, 2, CHUNK, COLS), jnp.float32),
            pltpu.VMEM((STEPS, 2, CHUNK, COLS), jnp.float32),
            pltpu.VMEM((CHUNKS, CHUNK + SCALE_ROWS, COLS), jnp.int16),
            pltpu.VMEM((STEPS, CHUNK + SCALE_ROWS, COLS), jnp.int16),
        ]
        + [dma((STEPS,))] * 8
        + [dma((2 * STEPS,))] * 2
        + [dma((STEPS,))] * 2
        + [dma, dma, dma((4,)), dma((4,)), dma((6,)), dma((10,)), dma((16,))],
        compiler_params=pltpu.CompilerParams(
            collective_id=0, has_side_effects=True, vmem_limit_bytes=56 * 1024 * 1024
        ),
        cost_estimate=pl.CostEstimate(
            flops=3 * 2 * ROWS * 1024 * 1024,
            bytes_accessed=4 * 1024 * 1024,
            transcendentals=0,
        ),
    )(tile_sizes, screen_ov.T, screen_vv, coupling, denominators, integrals)


def solution(mesh):
    in_specs = (P("blk", "bcast"), P("blk", "bcast"), P("bcast", "blk"), P(), P(), P())
    out_specs = P("blk", "bcast")
    return jax.shard_map(local, mesh=mesh, in_specs=in_specs, out_specs=out_specs, check_vma=False)
```

```python
import jax
import jax.numpy as jnp
from jax import lax
from jax.experimental import pallas as pl
from jax.experimental.pallas import tpu as pltpu
from jax.sharding import PartitionSpec as P

TILE = 128
ROW_TILE = 128
ITERS = 3
MESH = pl.DeviceIdType.MESH

ROWS = 1024
COLS = 256
CHUNK = 128
CHUNKS = ROWS // CHUNK
SPLIT = ROW_TILE // CHUNK
STEPS = ITERS * CHUNKS
HALF = CHUNK // 2
SCALE_ROWS = 16
FINAL = 4
SECOND = 2
FORWARD = 6
RING = 4


def device(x, y, z, core):
    x, y, z, core = x % 4, y % 4, z % 4, core % 2
    return (x * 2 + z % 2, ((z // 2) * 4 + y) * 2 + core)


def kernel(
    sizes_hbm,
    ov_hbm,
    vv_hbm,
    coupling_hbm,
    den_hbm,
    integrals_hbm,
    out_hbm,
    sizes_ref,
    ov_ref,
    vv_ref,
    coupling_ref,
    den_ref,
    integrals_ref,
    loaded,
    result,
    stored,
    weight,
    amp,
    swap,
    unit,
    ring,
    table,
    sib_out,
    own,
    sib_in,
    z_out,
    z_in,
    up_send,
    down_send,
    up_recv,
    down_recv,
    fup_send,
    fdown_send,
    fup_recv,
    fdown_recv,
    sib_send,
    sib_recv,
    z_send,
    z_recv,
    swap_send,
    swap_recv,
    ring_send,
    ring_recv,
    o_send,
    s_send,
    t_recv,
):
    blk = lax.axis_index("blk")
    bcast = lax.axis_index("bcast")
    x, zl = blk // 2, blk % 2
    zh, y, core = bcast // 8, (bcast // 2) % 4, bcast % 2
    z = zh * 2 + zl
    up = device(x, y + 1, z, core)
    down = device(x, y + 3, z, core)
    sibling = device(x, y, z, core + 1)
    across = device(x, y, z + 2, core)
    x_pair, x_out = x + 1 - 2 * (x % 2), x - 1 + 2 * (x % 2)
    z_mate, z_next = z + 1 - 2 * zl, z - 1 + 2 * zl
    pair_x = device(x_pair, y, z, core)
    out_x = device(x_out + 4, y, z, core)
    pair_z = device(x, y, z_mate, core)
    out_z = device(x, y, z_next + 4, core)
    right = device(x + 1, y, z, core)
    left = device(x + 3, y, z, core)
    inside = (x // 2) == zh
    outside = jnp.logical_not(inside)

    loads = [
        pltpu.make_async_copy(src, dst, loaded.at[n])
        for n, (src, dst) in enumerate(
            (
                (vv_hbm, vv_ref),
                (integrals_hbm, integrals_ref),
                (sizes_hbm, sizes_ref),
                (ov_hbm, ov_ref),
                (coupling_hbm, coupling_ref),
                (den_hbm, den_ref),
            )
        )
    ]
    barrier = pltpu.get_barrier_semaphore()
    for dev in (up, down, sibling, across, pair_x, out_x, pair_z, out_z):
        pl.semaphore_signal(barrier, inc=1, device_id=dev, device_id_type=MESH)
    for load in loads:
        load.start()

    def screened(h, ref):
        for j in range(2):
            for i in range(2):
                keep = vv_ref[bcast * 2 + i, blk * 4 + h * 2 + j].astype(jnp.float32)
                at = pl.ds(pl.multiple_of((h * 2 + j) * TILE, TILE), TILE)
                part = integrals_ref[pl.ds(i * TILE, TILE), at].astype(jnp.float32)
                ref[pl.ds(j * TILE, TILE), pl.ds(i * TILE, TILE)] = jnp.transpose(
                    part * keep
                ).astype(jnp.bfloat16)

    loads[0].wait()
    loads[1].wait()
    screened(1 - core, swap)
    screened(core, ring.at[x])

    def rows_of(k):
        return pl.ds(pl.multiple_of(k * CHUNK, CHUNK), CHUNK)

    def first_amplitudes(k):
        lane = lax.broadcasted_iota(jnp.int32, (CHUNK, COLS), 1)
        size0, size1 = sizes_ref[bcast * 2], sizes_ref[bcast * 2 + 1]
        ov0 = ov_ref[bcast * 2, blk * 8 + k // SPLIT]
        ov1 = ov_ref[bcast * 2 + 1, blk * 8 + k // SPLIT]
        live0 = jnp.where(lane < size0, ov0, 0)
        live1 = jnp.where(lane - TILE < size1, ov1, 0)
        keep = jnp.where(lane < TILE, live0, live1).astype(jnp.float32)
        w = keep / den_ref[rows_of(k), :]
        weight[rows_of(k), :] = w
        amp[0, y, rows_of(k), :] = (coupling_ref[rows_of(k), :] * w).astype(jnp.bfloat16)

    def part_of(t, owner, k, offset, length):
        start = pl.multiple_of(k * CHUNK + offset, HALF)
        return amp.at[t, owner, pl.ds(start, length), :]

    def remote(ref, target, send, recv):
        return pltpu.make_async_remote_copy(
            src_ref=ref, dst_ref=ref, send_sem=send, recv_sem=recv,
            device_id=target, device_id_type=MESH,
        )

    def send_up(s):
        ref = part_of(s // CHUNKS, y, s % CHUNKS, 0, CHUNK)
        return remote(ref, up, up_send.at[s], up_recv.at[s])

    def send_down(s):
        ref = part_of(s // CHUNKS, y, s % CHUNKS, 0, CHUNK)
        return remote(ref, down, down_send.at[s], down_recv.at[s])

    below, above, far = (y + 3) % RING, (y + 1) % RING, (y + 2) % RING

    def from_below(s):
        ref = part_of(s // CHUNKS, below, s % CHUNKS, 0, CHUNK)
        return remote(ref, up, up_send.at[s], up_recv.at[s])

    def from_above(s):
        ref = part_of(s // CHUNKS, above, s % CHUNKS, 0, CHUNK)
        return remote(ref, down, down_send.at[s], down_recv.at[s])

    def pass_up(s):
        ref = part_of(s // CHUNKS, below, s % CHUNKS, 0, HALF)
        return remote(ref, up, fup_send.at[s], fup_recv.at[s])

    def pass_down(s):
        ref = part_of(s // CHUNKS, above, s % CHUNKS, HALF, HALF)
        return remote(ref, down, fdown_send.at[s], fdown_recv.at[s])

    def far_from_below(s):
        ref = part_of(s // CHUNKS, far, s % CHUNKS, 0, HALF)
        return remote(ref, up, fup_send.at[s], fup_recv.at[s])

    def far_from_above(s):
        ref = part_of(s // CHUNKS, far, s % CHUNKS, HALF, HALF)
        return remote(ref, down, fdown_send.at[s], fdown_recv.at[s])

    def to_sibling(s, part):
        return pltpu.make_async_remote_copy(
            src_ref=sib_out.at[s % CHUNKS, part], dst_ref=sib_in.at[s, part],
            send_sem=sib_send.at[s * 2 + part], recv_sem=sib_recv.at[s * 2 + part],
            device_id=sibling, device_id_type=MESH,
        )

    def to_across(s):
        return pltpu.make_async_remote_copy(
            src_ref=z_out.at[s % CHUNKS], dst_ref=z_in.at[s],
            send_sem=z_send.at[s], recv_sem=z_recv.at[s],
            device_id=across, device_id_type=MESH,
        )

    def start_ring(s):
        send_up(s).start()
        send_down(s).start()

    def forward(s):
        from_below(s).wait_recv()
        pass_up(s).start()
        from_above(s).wait_recv()
        pass_down(s).start()

    def gathered(s):
        far_from_below(s).wait_recv()
        far_from_above(s).wait_recv()

    def product(s, part):
        t, k = s // CHUNKS, s % CHUNKS
        block = 2 * (zh if part else 1 - zh)
        lhs = jnp.concatenate([amp[t, o, rows_of(k), :] for o in range(RING)], axis=1)
        sib_out[k, part] = jnp.dot(
            lhs, table[block + 1 - core], preferred_element_type=jnp.float32
        )
        to_sibling(s, part).start()
        own[k, part] = jnp.dot(
            lhs, table[block + core], preferred_element_type=jnp.float32
        )

    def store(k):
        rows = rows_of(k)
        return pltpu.make_async_copy(
            result.at[rows, :], out_hbm.at[rows, :], stored.at[k]
        )

    def reduce_core(s):
        k = s % CHUNKS
        to_sibling(s, 0).wait()
        partial = own[k, 0] + sib_in[s, 0]
        most = jnp.max(jnp.abs(partial), axis=0, keepdims=True)
        log = jnp.floor(jnp.log2(jnp.maximum(most, 1e-30)) * 128.0) + 2.0
        coded = jnp.round(partial * (32766.0 * jnp.exp2(log * (-1.0 / 128.0))))
        z_out[k, pl.ds(0, CHUNK), :] = coded.astype(jnp.int32).astype(jnp.int16)
        logs = jnp.broadcast_to(log.astype(jnp.int32), (SCALE_ROWS, COLS))
        z_out[k, pl.ds(CHUNK, SCALE_ROWS), :] = logs.astype(jnp.int16)
        to_across(s).start()

    def finish(s):
        t, k = s // CHUNKS, s % CHUNKS
        to_sibling(s, 1).wait()
        to_across(s).wait()
        logs = z_in[s, pl.ds(CHUNK, SCALE_ROWS), :].astype(jnp.int32).astype(jnp.float32)
        scale = jnp.exp2(logs * (1.0 / 128.0))[:1] * (1.0 / 32766.0)
        coded = z_in[s, pl.ds(0, CHUNK), :].astype(jnp.int32).astype(jnp.float32)
        ladder = own[k, 1] + sib_in[s, 1] + coded * scale
        value = (coupling_ref[rows_of(k), :] + ladder) * weight[rows_of(k), :]

        @pl.when(t < ITERS - 1)
        def _():
            amp[t + 1, y, rows_of(k), :] = value.astype(jnp.bfloat16)
            start_ring(s + CHUNKS)

        @pl.when(t == ITERS - 1)
        def _():
            result[rows_of(k), :] = value
            store(k).start()

        send_up(s).wait_send()
        send_down(s).wait_send()
        pass_up(s).wait_send()
        pass_down(s).wait_send()

    def slot_of(first_core, zh_of, parity, zl_of):
        return (zh_of * 2 + first_core) * 4 + parity * 2 + zl_of

    def at_slot(slot):
        start = pl.multiple_of((slot % 4) * COLS, COLS)
        return table.at[slot // 4, pl.ds(start, COLS), :]

    def unit_copy(src, slot, send, target):
        return pltpu.make_async_remote_copy(
            src_ref=src, dst_ref=at_slot(slot), send_sem=send, recv_sem=t_recv.at[slot],
            device_id=target, device_id_type=MESH,
        )

    def arrived(slot):
        unit_copy(at_slot(slot), slot, swap_send, sibling).wait_recv()

    to_swap = pltpu.make_async_remote_copy(
        src_ref=swap, dst_ref=unit, send_sem=swap_send, recv_sem=swap_recv,
        device_id=sibling, device_id_type=MESH,
    )
    parity = x % 2

    def ring_part(owner, half):
        owner = (owner + 4) % 4
        if half is None:
            return ring.at[owner]
        return ring.at[owner, pl.ds(half * TILE, TILE), :]

    def ring_copy(owner, half, n, target):
        ref = ring_part(owner, half)
        return remote(ref, target, ring_send.at[n], ring_recv.at[n])

    def o_slot(owner):
        return slot_of(core, zh, owner % 2, zl)

    def over_z(n):
        owner = (x + (0, 3, 1, 2)[n]) % 4
        target = tuple(
            jnp.where(owner // 2 == zh, a, b) for a, b in zip(pair_z, out_z)
        )
        return unit_copy(ring.at[owner], o_slot(owner), o_send.at[n], target)

    def o_pass(n):
        slot = slot_of(core, 1 - zh, n, 1 - zl)
        return unit_copy(at_slot(slot), slot, o_send.at[4 + n], pair_z)

    s_slots = [
        lambda par, a=a, b=b: slot_of(1 - core, a, par, b)
        for a, b in ((zh, zl), (zh, 1 - zl), (1 - zh, 1 - zl), (1 - zh, zl))
    ]
    first_target = tuple(jnp.where(inside, a, b) for a, b in zip(pair_z, out_z))
    s_first = unit_copy(unit, s_slots[0](parity), s_send.at[0], first_target)
    s_pass = unit_copy(
        at_slot(s_slots[2](parity)), s_slots[2](parity), s_send.at[1], pair_z
    )

    def s_inside(n, k):
        slot = s_slots[n](parity)
        src = unit if n == 0 else at_slot(slot)
        return unit_copy(src, slot, s_send.at[2 + 2 * n + k], (pair_x, out_x)[k])

    def s_outside(n):
        slot = s_slots[n](1 - parity)
        return unit_copy(at_slot(slot), slot, s_send.at[2 + 2 * n], pair_x)

    def s_start(n):
        s_inside(n, 1).start()
        s_inside(n, 0).start()

    def s_relay(n):
        arrived(s_slots[n](1 - parity))
        s_outside(n).start()

    def forwards(eighth):
        @pl.loop(eighth * (CHUNKS // 8), (eighth + 1) * (CHUNKS // 8))
        def _(k):
            forward(k)

    for load in loads[2:]:
        load.wait()

    @pl.loop(0, CHUNKS)
    def _(k):
        first_amplitudes(k)

    pl.semaphore_wait(barrier, 8)
    to_swap.start()
    ring_copy(x, None, 0, right).start()
    ring_copy(x, None, 1, left).start()
    over_z(0).start()
    start_ring(0)

    to_swap.wait_recv()
    s_first.start()

    @pl.when(inside)
    def _():
        s_start(0)
        table[(zh * 2 + 1 - core), pl.ds(pl.multiple_of((parity * 2 + zl) * COLS, COLS), COLS), :] = unit[...]

    @pl.loop(1, CHUNKS // 2)
    def _(k):
        start_ring(k)

    ring_copy(x + 3, None, 0, right).wait_recv()
    ring_copy(x + 3, 0, 2, right).start()
    over_z(1).start()
    ring_copy(x + 1, None, 1, left).wait_recv()
    ring_copy(x + 1, 1, 3, left).start()
    over_z(2).start()

    @pl.loop(CHUNKS // 2, CHUNKS)
    def _(k):
        start_ring(k)

    forwards(0)

    @pl.when(inside)
    def _():
        arrived(s_slots[1](parity))
        s_start(1)
        arrived(s_slots[2](parity))
        s_pass.start()
        s_start(2)

    @pl.when(outside)
    def _():
        s_relay(0)

    ring_copy(x + 2, 0, 2, right).wait_recv()
    ring_copy(x + 2, 1, 3, left).wait_recv()
    over_z(3).start()
    for p in range(2):
        owner = 2 * zh + p
        table[zh * 2 + core, pl.ds(pl.multiple_of((p * 2 + zl) * COLS, COLS), COLS), :] = ring[owner]
    forwards(1)
    forwards(2)
    pl.when(outside)(lambda: s_relay(1))
    forwards(3)

    @pl.when(inside)
    def _():
        arrived(s_slots[3](parity))
        s_start(3)

    pl.when(outside)(lambda: s_relay(2))
    for n in range(2):
        which = (parity + n) % 2
        arrived(slot_of(core, 1 - zh, which, 1 - zl))
        o_pass(which).start()
    pl.when(outside)(lambda: s_relay(3))

    @pl.loop(4, CHUNKS)
    def _(k):
        forward(k)

    from_pair = jnp.where(inside, 1 - parity, parity)
    for n in range(2):
        arrived(slot_of(core, 1 - zh, n, zl))
        arrived(s_slots[2 + n](from_pair))
    gathered(0)
    product(0, 0)
    gathered(1)
    product(1, 0)
    reduce_core(0)
    for n in range(2):
        arrived(slot_of(core, zh, n, 1 - zl))
        arrived(s_slots[n](from_pair))

    def tick_of(tick, lag):
        return jnp.logical_and(tick >= lag, tick < STEPS + lag)

    @pl.loop(2, STEPS + FINAL)
    def _(tick):
        @pl.when(tick_of(tick, FINAL))
        def _():
            finish(tick - FINAL)

        @pl.when(tick_of(tick, 1))
        def _():
            reduce_core(tick - 1)

        @pl.when(jnp.logical_and(tick >= FORWARD, tick < STEPS - CHUNKS + FORWARD))
        def _():
            forward(tick - FORWARD + CHUNKS)

        @pl.when(tick < STEPS)
        def _():
            gathered(tick)
            product(tick, 0)

        @pl.when(tick_of(tick, SECOND))
        def _():
            product(tick - SECOND, 1)

    for k in range(CHUNKS):
        store(k).wait()
    to_swap.wait_send()
    for n, (owner, half) in enumerate(((x, None), (x, None), (x + 3, 0), (x + 1, 1))):
        ring_copy(owner, half, n, right).wait_send()
    for n in range(4):
        over_z(n).wait_send()
    o_pass(0).wait_send()
    o_pass(1).wait_send()
    s_first.wait_send()

    @pl.when(inside)
    def _():
        s_pass.wait_send()
        for n in range(4):
            for k in range(2):
                s_inside(n, k).wait_send()

    @pl.when(outside)
    def _():
        for n in range(4):
            s_outside(n).wait_send()


def local(coupling, denominators, integrals, tile_sizes, screen_ov, screen_vv):
    dma = pltpu.SemaphoreType.DMA
    anywhere = pl.BlockSpec(memory_space=pl.ANY)
    return pl.pallas_call(
        kernel,
        out_shape=jax.ShapeDtypeStruct((ROWS, COLS), jnp.float32),
        in_specs=[anywhere] * 6,
        out_specs=anywhere,
        scratch_shapes=[
            pltpu.SMEM((32,), jnp.int32),
            pltpu.SMEM((32, 64), jnp.int32),
            pltpu.SMEM((32, 32), jnp.int32),
            pltpu.VMEM((ROWS, COLS), jnp.float32),
            pltpu.VMEM((ROWS, COLS), jnp.float32),
            pltpu.VMEM((COLS, 2 * COLS), jnp.bfloat16),
            dma((6,)),
            pltpu.VMEM((ROWS, COLS), jnp.float32),
            dma((CHUNKS,)),
            pltpu.VMEM((ROWS, COLS), jnp.float32),
            pltpu.VMEM((ITERS, RING, ROWS, COLS), jnp.bfloat16),
            pltpu.VMEM((COLS, COLS), jnp.bfloat16),
            pltpu.VMEM((COLS, COLS), jnp.bfloat16),
            pltpu.VMEM((4, COLS, COLS), jnp.bfloat16),
            pltpu.VMEM((4, RING * COLS, COLS), jnp.bfloat16),
            pltpu.VMEM((CHUNKS, 2, CHUNK, COLS), jnp.float32),
            pltpu.VMEM((CHUNKS, 2, CHUNK, COLS), jnp.float32),
            pltpu.VMEM((STEPS, 2, CHUNK, COLS), jnp.float32),
            pltpu.VMEM((CHUNKS, CHUNK + SCALE_ROWS, COLS), jnp.int16),
            pltpu.VMEM((STEPS, CHUNK + SCALE_ROWS, COLS), jnp.int16),
        ]
        + [dma((STEPS,))] * 8
        + [dma((2 * STEPS,))] * 2
        + [dma((STEPS,))] * 2
        + [dma, dma, dma((4,)), dma((4,)), dma((6,)), dma((10,)), dma((16,))],
        compiler_params=pltpu.CompilerParams(
            collective_id=0, has_side_effects=True, vmem_limit_bytes=56 * 1024 * 1024
        ),
        cost_estimate=pl.CostEstimate(
            flops=3 * 2 * ROWS * 1024 * 1024,
            bytes_accessed=4 * 1024 * 1024,
            transcendentals=0,
        ),
    )(tile_sizes, screen_ov.T, screen_vv, coupling, denominators, integrals)


def solution(mesh):
    in_specs = (P("blk", "bcast"), P("blk", "bcast"), P("bcast", "blk"), P(), P(), P())
    out_specs = P("blk", "bcast")
    return jax.shard_map(local, mesh=mesh, in_specs=in_specs, out_specs=out_specs, check_vma=False)
```
